32 devices in a mesh: sector: 4 (over y, core), dom: 8 (over z, x).
Axes of the slice: x: 2, y: 2, z: 4, core: 2. Of those that a mesh axis runs over, the one named last changes fastest.
Arguments:
- amplitudes: float32 [64, 48], replicated, may hold values from -0.3 to 0.3
- mode_shapes: float32 [48, 3, 32768], P(None, None, ('sector', 'dom')), may hold values from -6 to 6
- shape_grads: float32 [8, 3, 32768], P(None, None, ('sector', 'dom')), may hold values from -2.4 to 2.4
- lame_params: float32 [2, 32768], P(None, ('sector', 'dom')), may hold values from 0.5 to 2
- connectivity: int32 [8, 32768], P(None, ('sector', 'dom')), may hold values from -1 to 1791, as said below
- dom_sends: int32 [2, 8192], P(None, ('sector', 'dom')), may hold values from -1 to 1023, as said below
- sector_sends: int32 [2, 4096], P(None, ('sector', 'dom')), may hold values from -1 to 1023, as said below
Outputs:
- nodal_force: float32 [64, 3, 32768], P(None, None, ('sector', 'dom'))
- modal_force: float32 [64, 48], replicated
The draws below stay inside these ranges and needn't reach their ends.
Inputs may be any that keep to these rules, and one draw needn't show every extreme that they name: `connectivity`: in each device's block, the live elements come first and the padding element slots after them hold -1 in all 8 rows; a live slot names a slot of the device's extended table. Some device has all 1024 slots live. `dom_sends`: each device's row lists its own node numbers first, then -1; a row holds 128 to 256 live entries, and some row is full. `sector_sends`: each device's row lists its own node numbers first, then -1; a row holds 64 to 128 live entries, and some row is full.
All inputs are finite; a program needn't handle non-finite values.
Results may differ from the reference program's by a relative error of at most 0.0003.
Values sent between devices are 32-bit elements; how exact they have to be, the bound alone decides.
No kernel may reach another device: no remote copies, remote signals or barrier semaphores. Data moves between devices by JAX's collectives and lax.ppermute only.
A program may use at most 64 MiB of HBM per device.

```python
import math
import jax
import jax.numpy as jnp
from jax import lax

COMBOS = 64
MODES = 48
NODE_DEV = 1024
ELEM_DEV = 1024
IF_DOM = 256
IF_SEC = 128
EXT_NODES = 1792
NODES = 32768
ELEMENTS = 32768
N_SECTOR = 4
N_DOM = 8


def padded_lists(key, list_width):
    device_total = NODES // NODE_DEV
    key_live, key_full, key_nodes = jax.random.split(key, 3)
    live_slots = jax.random.randint(key_live, (2 * device_total,), list_width // 2, list_width + 1)
    chosen = jax.random.randint(key_full, (), 0, 2 * device_total)
    live_slots = jnp.where(jnp.arange(2 * device_total) == chosen, list_width, live_slots).reshape(2, device_total)
    picked = jax.random.randint(key_nodes, (2, device_total, list_width), 0, NODE_DEV)
    positions = jnp.arange(list_width)[None, None, :]
    lists_out = jnp.where(positions < live_slots[:, :, None], picked, -1)
    return lists_out.reshape(2, device_total * list_width).astype(jnp.int32)


def draw_dom_sends(key, part):
    return padded_lists(jax.random.fold_in(key, 11), IF_DOM)


def draw_sector_sends(key, part):
    return padded_lists(jax.random.fold_in(key, 23), IF_SEC)


def draw_connectivity(key, part):
    device_total = ELEMENTS // ELEM_DEV
    key_load, key_full, key_own, key_halo, key_pick = jax.random.split(jax.random.fold_in(key, 37), 5)
    loads = ELEM_DEV * 7 // 8 + ELEM_DEV // 32 * jax.random.randint(key_load, (device_total,), 0, 5)
    chosen = jax.random.randint(key_full, (), 0, device_total)
    loads = jnp.where(jnp.arange(device_total) == chosen, ELEM_DEV, loads)
    own_refs = jax.random.randint(key_own, (8, device_total, ELEM_DEV), 0, NODE_DEV)
    halo_refs = jax.random.randint(key_halo, (8, device_total, ELEM_DEV), NODE_DEV, EXT_NODES)
    picks = jax.random.randint(key_pick, (8, device_total, ELEM_DEV), 0, 5)
    refs = jnp.where(picks == 0, halo_refs, own_refs)
    live_mask = jnp.arange(ELEM_DEV)[None, None, :] < loads[None, :, None]
    return jnp.where(live_mask, refs, -1).reshape(8, ELEMENTS).astype(jnp.int32)


def level_of(own_key, shape, cuts, least, largest):
    def one(position, parts):
        draws = jax.random.uniform(jax.random.fold_in(jax.random.fold_in(own_key, 6), position), (parts,), jnp.float32, least / len(cuts), largest / len(cuts))
        return jnp.repeat(jnp.exp(draws), shape[position] // parts).reshape((-1,) + (1,) * (len(shape) - position - 1))

    level = one(*cuts[0])
    for cut in cuts[1:]:
        level = level * one(*cut)
    return level


def normal_values(own_key, extent, deviation, reach, shards=(), held_as=jnp.bfloat16):
    gain = level_of(own_key, extent, shards, -0.22, 0.18) if shards else 1.0
    values = jax.random.normal(own_key, extent, jnp.float32) * deviation * gain
    return jnp.minimum(jnp.maximum(values, -reach), reach).astype(held_as)


def setup_inputs(seed: int = 0) -> dict:
    key_list = jax.random.split(jax.random.key(seed), 8)
    return {
        "amplitudes": normal_values(key_list[0], (COMBOS, MODES), 0.05, 0.3, (), jnp.float32),
        "mode_shapes": normal_values(key_list[1], (MODES, 3, NODES), 1.0, 6.0, ((2, 32),), jnp.float32),
        "shape_grads": normal_values(key_list[2], (8, 3, ELEMENTS), 0.4, 2.4, ((2, 32),), jnp.float32),
        "lame_params": jnp.clip(jnp.exp(math.log(2.0) - 1.3862944 * jax.random.uniform(key_list[3], (2, ELEMENTS), jnp.float32) ** level_of(key_list[3], (2, ELEMENTS), ((1, 32),), -0.2, 0.2)), 0.5, 2.0),
        "connectivity": draw_connectivity(jax.random.fold_in(key_list[7], 71), 0),
        "dom_sends": draw_dom_sends(jax.random.fold_in(key_list[7], 71), 0),
        "sector_sends": draw_sector_sends(jax.random.fold_in(key_list[7], 71), 0),
    }


def take_slots(node_table, send_lists):
    slot_width = node_table.shape[1]
    slot_index = jnp.where(send_lists < 0, slot_width, send_lists).reshape(-1)
    return jnp.take(node_table, slot_index, axis=1, mode='fill', fill_value=0.0)

def add_slots(node_table, send_lists, add_values):
    slot_width = node_table.shape[1]
    slot_index = jnp.where(send_lists < 0, slot_width, send_lists).reshape(-1)
    return node_table.at[:, slot_index].add(add_values, mode='drop')

def element_forces(accum, extended, connect, gradients, lame):
    ext_width = extended.shape[1]
    combo_total = extended.shape[0] // 3
    elem_total = connect.shape[1]
    slot_index = jnp.where(connect < 0, ext_width, connect).reshape(-1)
    corners = jnp.take(extended, slot_index, axis=1, mode='fill', fill_value=0.0).reshape(combo_total, 3, 8, elem_total)
    gradient = jnp.zeros((combo_total, 3, 3, elem_total), extended.dtype)
    for corner in range(8):
        gradient = gradient + corners[:, :, None, corner, :] * gradients[corner][None, None, :, :]
    quadratic = lax.optimization_barrier(jnp.sum(gradient[:, :, :, None, :] * gradient[:, :, None, :, :], axis=1))
    green_strain = 0.5 * (gradient + jnp.swapaxes(gradient, 1, 2) + quadratic)
    strain_trace = green_strain[:, 0, 0] + green_strain[:, 1, 1] + green_strain[:, 2, 2]
    identity = jnp.eye(3, dtype=extended.dtype)[None, :, :, None]
    stress = lame[0] * strain_trace[:, None, None, :] * identity + 2.0 * lame[1] * green_strain
    piola = stress + lax.optimization_barrier(jnp.sum(gradient[:, :, :, None, :] * stress[:, None, :, :, :], axis=2))
    corner_forces = jnp.stack([lax.optimization_barrier(jnp.sum(piola * gradients[corner][None, None, :, :], axis=2)) for corner in range(8)], axis=2)
    return accum.at[:, slot_index].add(corner_forces.reshape(3 * combo_total, 8 * elem_total), mode='drop')

def from_partitions(packet_rows, slot_width):
    below_part = jnp.concatenate([jnp.zeros_like(packet_rows[:, :1, :, slot_width:]), packet_rows[:, :-1, :, slot_width:]], axis=1)
    above_part = jnp.concatenate([packet_rows[:, 1:, :, :slot_width], jnp.zeros_like(packet_rows[:, :1, :, :slot_width])], axis=1)
    return (below_part, above_part)

def from_sectors(packet_rows, slot_width):
    below_part = jnp.roll(packet_rows[..., slot_width:], 1, axis=0)
    above_part = jnp.roll(packet_rows[..., :slot_width], -1, axis=0)
    return (below_part, above_part)

def reference(amplitudes, mode_shapes, shape_grads, lame_params, connectivity, dom_sends, sector_sends):
    device_total = N_SECTOR * N_DOM
    table_rows = 3 * COMBOS
    flat_width = 3 * NODE_DEV
    shapes_dev = mode_shapes.reshape(MODES, 3, device_total, NODE_DEV).transpose(2, 0, 1, 3).reshape(device_total, MODES, flat_width)
    displaced = jnp.einsum('cm,vmx->vcx', amplitudes, shapes_dev, precision=lax.Precision.HIGHEST).reshape(device_total, table_rows, NODE_DEV)
    dom_lists = dom_sends.reshape(2, device_total, IF_DOM).transpose(1, 0, 2)
    sec_lists = sector_sends.reshape(2, device_total, IF_SEC).transpose(1, 0, 2)
    dom_packets = jax.vmap(take_slots)(displaced, dom_lists).reshape(N_SECTOR, N_DOM, table_rows, 2 * IF_DOM)
    sec_packets = jax.vmap(take_slots)(displaced, sec_lists).reshape(N_SECTOR, N_DOM, table_rows, 2 * IF_SEC)
    dom_below, dom_above = from_partitions(dom_packets, IF_DOM)
    sec_below, sec_above = from_sectors(sec_packets, IF_SEC)
    extended = jnp.concatenate([displaced.reshape(N_SECTOR, N_DOM, table_rows, NODE_DEV), dom_below, dom_above, sec_below, sec_above], axis=-1)
    extended = extended.reshape(device_total, table_rows, EXT_NODES)
    connect_dev = connectivity.reshape(8, device_total, ELEM_DEV).transpose(1, 0, 2)
    grads_dev = shape_grads.reshape(8, 3, device_total, ELEM_DEV).transpose(2, 0, 1, 3)
    lame_dev = lame_params.reshape(2, device_total, ELEM_DEV).transpose(1, 0, 2)

    def per_device(inputs_dev):
        table_dev, connect_one, grads_one, lame_one = inputs_dev
        start_table = jnp.zeros((table_rows, EXT_NODES), table_dev.dtype)
        return element_forces(start_table, table_dev, connect_one, grads_one, lame_one)
    slot_forces = lax.map(per_device, (extended, connect_dev, grads_dev, lame_dev))
    own_forces = slot_forces[..., :NODE_DEV]
    dom_back = slot_forces[..., NODE_DEV:NODE_DEV + 2 * IF_DOM].reshape(N_SECTOR, N_DOM, table_rows, 2 * IF_DOM)
    sec_back = slot_forces[..., NODE_DEV + 2 * IF_DOM:].reshape(N_SECTOR, N_DOM, table_rows, 2 * IF_SEC)
    back_below, back_above = from_partitions(dom_back, IF_DOM)
    returned_dom = jnp.concatenate([back_below, back_above], axis=-1).reshape(device_total, table_rows, 2 * IF_DOM)
    own_forces = jax.vmap(add_slots)(own_forces, dom_lists, returned_dom)
    back_below, back_above = from_sectors(sec_back, IF_SEC)
    returned_sec = jnp.concatenate([back_below, back_above], axis=-1).reshape(device_total, table_rows, 2 * IF_SEC)
    own_forces = jax.vmap(add_slots)(own_forces, sec_lists, returned_sec)
    nodal_out = own_forces.reshape(device_total, COMBOS, 3, NODE_DEV).transpose(1, 2, 0, 3).reshape(COMBOS, 3, NODES)
    modal_sum = jnp.einsum('vcx,vmx->cm', own_forces.reshape(device_total, COMBOS, flat_width), shapes_dev, precision=lax.Precision.HIGHEST)
    return (nodal_out, modal_sum / math.sqrt(3.0 * NODES))
```

```python
import functools
import math

import jax
import jax.numpy as jnp
from jax import lax
from jax.experimental import pallas as pl
from jax.experimental.pallas import tpu as pltpu
from jax.sharding import PartitionSpec as P

F32 = jnp.float32
BF16 = jnp.bfloat16
I16 = jnp.int16
MIB = 1 << 20
LANES = 256
NN = (((1,), (0,)), ((), ()))
NT = (((1,), (1,)), ((), ()))


def dot(a, b, dims):
    return lax.dot_general(a, b, dims, preferred_element_type=F32)


def split(x):
    hi = x.astype(BF16)
    return hi, (x - hi.astype(F32)).astype(BF16)


def partners(count, even_up):
    out = []
    for i in range(count):
        up = (i % 2 == 0) == even_up
        out.append((i, i + 1 if up else i - 1))
    return out


def swap(x, axis, even_up, closed):
    count = lax.axis_size(axis)
    pairs = [(i, j) for i, j in partners(count, even_up) if closed or 0 <= j < count]
    return lax.ppermute(x, axis, [(i, j % count) for i, j in pairs])


def send_rows(par_ref, dom_ref, sec_ref):
    dom_odd = par_ref[0] == 1
    sec_odd = par_ref[1] == 1
    d0, d1 = dom_ref[0:1, :], dom_ref[1:2, :]
    s0, s1 = sec_ref[0:1, :], sec_ref[1:2, :]
    return [
        jnp.where(dom_odd, d0, d1),
        jnp.where(dom_odd, d1, d0),
        jnp.where(sec_odd, s0, s1),
        jnp.where(sec_odd, s1, s0),
    ]


def one_hot(row, node_total):
    ids = lax.broadcasted_iota(jnp.int32, (node_total, row.shape[1]), 0)
    return jnp.where(ids == row, 1.0, 0.0).astype(BF16)


def packet_kernel(par_ref, shapes_ref, dom_ref, sec_ref, *out_refs):
    node_total = shapes_ref.shape[2]
    modes = shapes_ref.shape[1]
    hot = [one_hot(r, node_total) for r in send_rows(par_ref, dom_ref, sec_ref)]
    for i in range(3):
        hi, lo = split(shapes_ref[i])
        for h, o in zip(hot, out_refs):
            o[i * modes : (i + 1) * modes, :] = dot(hi, h, NN) + dot(lo, h, NN)


def build_kernel(par_ref, shapes_ref, conn_ref, grads_ref, wh_ref, wl_ref, own_ref,
                 conn_s, grad_s, cs, ghs, gls, ios, phi_h, phi_l, *, dom_width, sec_width):
    node_total = shapes_ref.shape[2]
    modes = shapes_ref.shape[1]
    chunks = wh_ref.shape[0]
    conn = conn_ref[...]
    corner = lax.broadcasted_iota(jnp.int32, conn.shape, 0)
    grads = [grads_ref[j] for j in range(3)]
    total = list(grads)
    drop = jnp.zeros(conn.shape, jnp.bool_)
    for s in range(1, 8):
        same = pltpu.roll(conn, 8 - s, 0) == conn
        drop = drop | (same & (corner >= 8 - s))
        total = [t + jnp.where(same, pltpu.roll(g, 8 - s, 0), 0.0) for t, g in zip(total, grads)]
    conn_s[...] = jnp.where(drop, -1, conn)
    for j in range(3):
        grad_s[j] = total[j]
    for i in range(3):
        hi, lo = split(shapes_ref[i])
        phi_h[i * modes : (i + 1) * modes, :] = hi
        phi_l[i * modes : (i + 1) * modes, :] = lo
    ios[...] = lax.broadcasted_iota(jnp.int32, (8, LANES), 0).astype(I16)
    dom_odd, sec_odd = par_ref[0], par_ref[1]
    first = node_total
    segments = [(0, node_total, 0)]
    for width, odd in ((dom_width, dom_odd), (sec_width, sec_odd)):
        segments.append((first, width, first + (1 - odd) * width))
        segments.append((first + width, width, first + odd * width))
        first += 2 * width
    unit = 4

    def chunk(t, carry):
        e0 = pl.multiple_of(t * LANES, LANES)
        for a in range(8):
            cs[a] = jnp.broadcast_to(conn_s[a : a + 1, pl.ds(e0, LANES)], (8, LANES)).astype(I16)
            for j in range(3):
                g = jnp.broadcast_to(grad_s[j, a : a + 1, pl.ds(e0, LANES)], (8, LANES))
                hi, lo = split(g)
                ghs[j * 8 + a] = hi
                gls[j * 8 + a] = lo

        for row0, rows, slot0 in segments:

            def block(s, carry, row0=row0, slot0=slot0):
                s0 = pl.multiple_of(s * (8 * unit), 8 * unit)
                for k in range(unit):
                    ids = ios[...] + (slot0 + s0 + 8 * k).astype(I16)
                    hi = [jnp.zeros((8, LANES), BF16)] * 3
                    lo = list(hi)
                    for a in range(8):
                        m = cs[a] == ids
                        for j in range(3):
                            hi[j] = jnp.where(m, ghs[j * 8 + a], hi[j])
                            lo[j] = jnp.where(m, gls[j * 8 + a], lo[j])
                    r = pl.ds(row0 + s0 + 8 * k, 8)
                    for j in range(3):
                        wh_ref[t, r, j * LANES : (j + 1) * LANES] = hi[j]
                        wl_ref[t, r, j * LANES : (j + 1) * LANES] = lo[j]
                return carry

            lax.fori_loop(0, rows // (8 * unit), block, 0)
        wh = wh_ref[t, 0:node_total, :]
        own_ref[t] = (
            dot(phi_h[...], wh, NN)
            + dot(phi_l[...], wh, NN)
            + dot(phi_h[...], wl_ref[t, 0:node_total, :], NN)
        )
        return carry

    lax.fori_loop(0, chunks, chunk, 0)


def element_kernel(amps_ref, lame_ref, own_ref, a_ref, b_ref, c_ref, d_ref, wh_ref, wl_ref,
                   ph_ref, pl_ref, modal_ref, hal_h, hal_l, disp):
    node_total = wh_ref.shape[1] - sum(r.shape[1] for r in (a_ref, b_ref, c_ref, d_ref))
    chunks = wh_ref.shape[0]
    modes, combos = amps_ref.shape
    col = 0
    for r in (a_ref, b_ref, c_ref, d_ref):
        hi, lo = split(r[...])
        hal_h[:, col : col + r.shape[1]] = hi
        hal_l[:, col : col + r.shape[1]] = lo
        col += r.shape[1]
    amp_h, amp_l = split(amps_ref[...].T)
    amp = jnp.concatenate([amp_h, amp_h, amp_l], axis=1)
    modal_ref[...] = jnp.zeros_like(modal_ref)

    def chunk(t, carry):
        e0 = pl.multiple_of(t * LANES, LANES)
        wh = wh_ref[t, node_total:, :]
        grad = (
            own_ref[t]
            + dot(hal_h[...], wh, NN)
            + dot(hal_l[...], wh, NN)
            + dot(hal_h[...], wl_ref[t, node_total:, :], NN)
        )
        gh, gl = split(grad)
        for i in range(3):
            r = slice(i * modes, (i + 1) * modes)
            disp[i] = dot(amp, jnp.concatenate([gh[r], gl[r], gh[r]], axis=0), NN)
        for half in range(LANES // 128):
            lam = jnp.broadcast_to(lame_ref[0:1, pl.ds(e0 + half * 128, 128)], (16, 128)) * 0.5
            mu = jnp.broadcast_to(lame_ref[1:2, pl.ds(e0 + half * 128, 128)], (16, 128))

            def rows(b, carry, half=half, lam=lam, mu=mu):
                r0 = pl.multiple_of(b * 16, 16)
                h = [
                    [disp[i, pl.ds(r0, 16), j * LANES + half * 128 : j * LANES + half * 128 + 128] for j in range(3)]
                    for i in range(3)
                ]
                s = {}
                for j in range(3):
                    for k in range(j, 3):
                        q = h[0][j] * h[0][k] + h[1][j] * h[1][k] + h[2][j] * h[2][k]
                        s[j, k] = (h[j][k] + h[k][j]) + q
                trace = lam * (s[0, 0] + s[1, 1] + s[2, 2])
                for j in range(3):
                    for k in range(j, 3):
                        v = mu * s[j, k]
                        v = v + trace if j == k else v
                        s[j, k] = s[k, j] = v
                for i in range(3):
                    for j in range(3):
                        p = s[i, j] + (h[i][0] * s[0, j] + h[i][1] * s[1, j] + h[i][2] * s[2, j])
                        hi, lo = split(p)
                        at = (t, pl.ds(i * combos + r0, 16), slice(j * LANES + half * 128, j * LANES + half * 128 + 128))
                        ph_ref[at] = hi
                        pl_ref[at] = lo
                return carry

            lax.fori_loop(0, combos // 16, rows, 0)
        acc = modal_ref[...]
        for i in range(3):
            r = slice(i * modes, (i + 1) * modes)
            c = slice(i * combos, (i + 1) * combos)
            both = dot(jnp.concatenate([gh[r], gl[r]], axis=0), ph_ref[t, c, :], NT)
            acc = acc + both[:modes] + both[modes:] + dot(gh[r], pl_ref[t, c, :], NT)
        modal_ref[...] = acc
        return carry

    lax.fori_loop(0, chunks, chunk, 0)


def force_rows(ph_ref, pl_ref, wh_ref, wl_ref, t, lo, hi):
    wh = wh_ref[t, lo:hi, :]
    return (
        dot(ph_ref[t], wh, NT) + dot(pl_ref[t], wh, NT) + dot(ph_ref[t], wl_ref[t, lo:hi, :], NT)
    )


def halo_kernel(ph_ref, pl_ref, wh_ref, wl_ref, *out_refs):
    chunks, slots, _ = wh_ref.shape
    first = slots - sum(o.shape[1] for o in out_refs)
    for o in out_refs:
        o[...] = jnp.zeros_like(o)

    def chunk(t, carry):
        part = force_rows(ph_ref, pl_ref, wh_ref, wl_ref, t, first, slots)
        col = 0
        for o in out_refs:
            o[...] += part[:, col : col + o.shape[1]]
            col += o.shape[1]
        return carry

    lax.fori_loop(0, chunks, chunk, 0)


def own_kernel(ph_ref, pl_ref, wh_ref, wl_ref, out_ref):
    node_total = out_ref.shape[1]
    out_ref[...] = jnp.zeros_like(out_ref)

    def chunk(t, carry):
        out_ref[...] += force_rows(ph_ref, pl_ref, wh_ref, wl_ref, t, 0, node_total)
        return carry

    lax.fori_loop(0, wh_ref.shape[0], chunk, 0)


def add_kernel(par_ref, own_ref, dom_ref, sec_ref, a_ref, b_ref, c_ref, d_ref, out_ref):
    node_total = own_ref.shape[1]
    combos = out_ref.shape[1]
    total = own_ref[...]
    for row, r in zip(send_rows(par_ref, dom_ref, sec_ref), (a_ref, b_ref, c_ref, d_ref)):
        hot = one_hot(row, node_total)
        hi, lo = split(r[...])
        total = total + dot(hi, hot, NT) + dot(lo, hot, NT)
    for i in range(3):
        out_ref[i] = total[i * combos : (i + 1) * combos]


def call(kernel, out_shape, args, scratch=(), vmem=24, smem=(), flops=0):
    vm = pl.BlockSpec(memory_space=pltpu.VMEM)
    sm = pl.BlockSpec(memory_space=pltpu.SMEM)
    many = isinstance(out_shape, (list, tuple))
    return pl.pallas_call(
        kernel,
        out_shape=out_shape,
        in_specs=[sm if i in smem else vm for i in range(len(args))],
        out_specs=[vm] * len(out_shape) if many else vm,
        scratch_shapes=list(scratch),
        compiler_params=pltpu.CompilerParams(vmem_limit_bytes=vmem * MIB),
        cost_estimate=pl.CostEstimate(flops=flops, bytes_accessed=1 << 20, transcendentals=0),
    )(*args)


def local(amplitudes, mode_shapes, shape_grads, lame_params, connectivity, dom_sends, sector_sends):
    modes, _, node_total = mode_shapes.shape
    combos = amplitudes.shape[0]
    elems = connectivity.shape[1]
    dom_width, sec_width = dom_sends.shape[1], sector_sends.shape[1]
    slots = node_total + 2 * (dom_width + sec_width)
    chunks = elems // LANES
    cols = 3 * LANES
    sds = jax.ShapeDtypeStruct
    widths = (dom_width, dom_width, sec_width, sec_width)
    parity = jnp.stack([lax.axis_index("dom") % 2, lax.axis_index("sector") % 2]).astype(jnp.int32)
    shapes = mode_shapes.transpose(1, 0, 2)
    grads = shape_grads.transpose(1, 0, 2)

    def exchange(a, b, c, d):
        return (
            swap(a, "dom", True, False),
            swap(b, "dom", False, False),
            swap(c, "sector", True, True),
            swap(d, "sector", False, True),
        )

    packets = call(
        packet_kernel,
        [sds((3 * modes, w), F32) for w in widths],
        (parity, shapes, dom_sends, sector_sends),
        smem=(0,),
    )
    halo = exchange(*packets)
    wh, wl, own_grad = call(
        functools.partial(build_kernel, dom_width=dom_width, sec_width=sec_width),
        [sds((chunks, slots, cols), BF16)] * 2 + [sds((chunks, 3 * modes, cols), F32)],
        (parity, shapes, connectivity, grads),
        scratch=[
            pltpu.VMEM((8, elems), jnp.int32),
            pltpu.VMEM((3, 8, elems), F32),
            pltpu.VMEM((8, 8, LANES), I16),
            pltpu.VMEM((24, 8, LANES), BF16),
            pltpu.VMEM((24, 8, LANES), BF16),
            pltpu.VMEM((8, LANES), I16),
            pltpu.VMEM((3 * modes, node_total), BF16),
            pltpu.VMEM((3 * modes, node_total), BF16),
        ],
        smem=(0,),
        flops=6 * 3 * modes * node_total * 3 * elems,
    )
    ph, pl_, modal = call(
        element_kernel,
        [sds((chunks, 3 * combos, cols), BF16)] * 2 + [sds((modes, combos), F32)],
        (amplitudes.T, lame_params, own_grad, *halo, wh, wl),
        scratch=[
            pltpu.VMEM((3 * modes, sum(widths)), BF16),
            pltpu.VMEM((3 * modes, sum(widths)), BF16),
            pltpu.VMEM((3, combos, cols), F32),
        ],
    )
    back = call(halo_kernel, [sds((3 * combos, w), F32) for w in widths], (ph, pl_, wh, wl))
    returned = exchange(*back)
    own = call(
        own_kernel,
        sds((3 * combos, node_total), F32),
        (ph, pl_, wh, wl),
        flops=6 * 3 * combos * node_total * 3 * elems,
    )
    forces = call(
        add_kernel,
        sds((3, combos, node_total), F32),
        (parity, own, dom_sends, sector_sends, *returned),
        smem=(0,),
    )
    for axis in ("sector", "dom"):
        count = lax.axis_size(axis)
        step = 1
        while step < count:
            modal = modal + lax.ppermute(modal, axis, [(i, i ^ step) for i in range(count)])
            step *= 2
    all_nodes = node_total * lax.axis_size("sector") * lax.axis_size("dom")
    return forces.transpose(1, 0, 2), modal.T / math.sqrt(3.0 * all_nodes)


def solution(mesh):
    placed = (
        P(),
        P(None, None, ("sector", "dom")),
        P(None, None, ("sector", "dom")),
        P(None, ("sector", "dom")),
        P(None, ("sector", "dom")),
        P(None, ("sector", "dom")),
        P(None, ("sector", "dom")),
    )
    return jax.shard_map(
        local,
        mesh=mesh,
        in_specs=placed,
        out_specs=(P(None, None, ("sector", "dom")), P()),
        check_vma=False,
    )
```

```python
import functools
import math

import jax
import jax.numpy as jnp
from jax import lax
from jax.experimental import pallas as pl
from jax.experimental.pallas import tpu as pltpu
from jax.sharding import PartitionSpec as P

F32 = jnp.float32
BF16 = jnp.bfloat16
I16 = jnp.int16
MIB = 1 << 20
LANES = 256
NN = (((1,), (0,)), ((), ()))
NT = (((1,), (1,)), ((), ()))


def dot(a, b, dims):
    return lax.dot_general(a, b, dims, preferred_element_type=F32)


def split(x):
    hi = x.astype(BF16)
    return hi, (x - hi.astype(F32)).astype(BF16)


def partners(count, even_up):
    out = []
    for i in range(count):
        up = (i % 2 == 0) == even_up
        out.append((i, i + 1 if up else i - 1))
    return out


def swap(x, axis, even_up, closed):
    count = lax.axis_size(axis)
    pairs = [(i, j) for i, j in partners(count, even_up) if closed or 0 <= j < count]
    return lax.ppermute(x, axis, [(i, j % count) for i, j in pairs])


def parity():
    return lax.axis_index("dom") % 2, lax.axis_index("sector") % 2


def send_rows(dom_ref, sec_ref):
    dom_odd, sec_odd = (p == 1 for p in parity())
    d0, d1 = dom_ref[0:1, :], dom_ref[1:2, :]
    s0, s1 = sec_ref[0:1, :], sec_ref[1:2, :]
    return [
        jnp.where(dom_odd, d0, d1),
        jnp.where(dom_odd, d1, d0),
        jnp.where(sec_odd, s0, s1),
        jnp.where(sec_odd, s1, s0),
    ]


def one_hot(row, node_total):
    ids = lax.broadcasted_iota(jnp.int32, (node_total, row.shape[1]), 0)
    return jnp.where(ids == row, 1.0, 0.0).astype(BF16)


def packet_kernel(shapes_hbm, grads_hbm, conn_hbm, lame_hbm, dom_hbm, sec_hbm,
                  a_ref, b_ref, c_ref, d_ref, hot_ref, phi_ref, grads_ref, conn_ref, lame_ref,
                  shapes_ref, dom_ref, sec_ref, sems):
    pairs = [
        (dom_hbm, dom_ref),
        (sec_hbm, sec_ref),
        (shapes_hbm, shapes_ref),
        (grads_hbm, grads_ref),
        (conn_hbm, conn_ref),
        (lame_hbm, lame_ref),
    ]
    copies = [pltpu.make_async_copy(src, dst, sems.at[k]) for k, (src, dst) in enumerate(pairs)]
    for c in copies:
        c.start()
    node_total = shapes_ref.shape[2]
    modes = shapes_ref.shape[1]
    copies[0].wait()
    copies[1].wait()
    col = 0
    for row in send_rows(dom_ref, sec_ref):
        width = row.shape[1]
        hot_ref[:, col : col + width] = one_hot(row, node_total)
        col += width
    copies[2].wait()
    for i in range(3):
        hi, lo = split(shapes_ref[i])
        phi_ref[i * modes : (i + 1) * modes, :] = hi
        phi_ref[(3 + i) * modes : (4 + i) * modes, :] = lo
    half = 3 * modes
    col = 0
    for o in (a_ref, b_ref, c_ref, d_ref):
        width = o.shape[1]
        part = dot(phi_ref[...], hot_ref[:, col : col + width], NN)
        o[...] = part[:half] + part[half:]
        col += width
    for c in copies[3:]:
        c.wait()


def build_kernel(phi_ref, conn_ref, grads_ref, wh_ref, wl_ref, vh_ref, vl_ref, own_ref,
                 conn_s, grad_s, cs, ghs, gls, ios, bases, *, dom_width, sec_width):
    node_total = phi_ref.shape[1]
    half = phi_ref.shape[0] // 2
    chunks = wh_ref.shape[0]
    conn = conn_ref[...]
    corner = lax.broadcasted_iota(jnp.int32, conn.shape, 0)
    grads = [grads_ref[j] for j in range(3)]
    total = list(grads)
    drop = jnp.zeros(conn.shape, jnp.bool_)
    for s in range(1, 8):
        same = pltpu.roll(conn, 8 - s, 0) == conn
        drop = drop | (same & (corner >= 8 - s))
        total = [t + jnp.where(same, pltpu.roll(g, 8 - s, 0), 0.0) for t, g in zip(total, grads)]
    conn_s[...] = jnp.where(drop, -1, conn)
    for j in range(3):
        grad_s[j] = total[j]
    ios[...] = lax.broadcasted_iota(jnp.int32, (8, LANES), 0).astype(I16)
    run = 0
    first = node_total
    for width, odd in zip((dom_width, sec_width), parity()):
        for start in (first + (1 - odd) * width, first + odd * width):
            for k in range(width // sec_width):
                bases[run] = start + k * sec_width
                run += 1
        first += 2 * width
    runs_each = run // 3

    def units(hi_ref, lo_ref, t, row0, slot0, count):
        for k in range(count):
            ids = ios[...] + (slot0 + 8 * k).astype(I16)
            hi = [jnp.zeros((8, LANES), BF16)] * 3
            lo = list(hi)
            for a in range(8):
                m = cs[a] == ids
                for j in range(3):
                    hi[j] = jnp.where(m, ghs[j * 8 + a], hi[j])
                    lo[j] = jnp.where(m, gls[j * 8 + a], lo[j])
            r = pl.ds(row0 + 8 * k, 8)
            for j in range(3):
                hi_ref[t, r, j * LANES : (j + 1) * LANES] = hi[j]
                lo_ref[t, r, j * LANES : (j + 1) * LANES] = lo[j]

    unit = 8

    def chunk(t, carry):
        e0 = pl.multiple_of(t * LANES, LANES)
        for a in range(8):
            cs[a] = jnp.broadcast_to(conn_s[a : a + 1, pl.ds(e0, LANES)], (8, LANES)).astype(I16)
            for j in range(3):
                g = jnp.broadcast_to(grad_s[j, a : a + 1, pl.ds(e0, LANES)], (8, LANES))
                hi, lo = split(g)
                ghs[j * 8 + a] = hi
                gls[j * 8 + a] = lo

        def own_rows(s, carry):
            s0 = pl.multiple_of(s * (8 * unit), 8 * unit)
            units(wh_ref, wl_ref, t, s0, s0, unit)
            return carry

        lax.fori_loop(0, node_total // (8 * unit), own_rows, 0)

        def halo_rows(j, carry):
            col = pl.ds(pl.multiple_of(j * LANES, LANES), LANES)
            part = dot(phi_ref[...], wh_ref[t, :, col], NN)
            own_ref[t, :, col] = part[:half] + part[half:] + dot(phi_ref[0:half], wl_ref[t, :, col], NN)
            for k in range(runs_each):
                run = j * runs_each + k
                row0 = pl.multiple_of(run * sec_width, sec_width)
                units(vh_ref, vl_ref, t, row0, bases[run], sec_width // 8)
            return carry

        lax.fori_loop(0, 3, halo_rows, 0)
        return carry

    lax.fori_loop(0, chunks, chunk, 0)


def element_kernel(amps_ref, lame_ref, own_ref, a_ref, b_ref, c_ref, d_ref, vh_ref, vl_ref,
                   pio_ref, modal_ref, hal, disp, grad_h, grad_l):
    chunks = vh_ref.shape[0]
    modes, combos = amps_ref.shape
    half = 3 * modes
    col = 0
    for r in (a_ref, b_ref, c_ref, d_ref):
        hi, lo = split(r[...])
        hal[0:half, col : col + r.shape[1]] = hi
        hal[half:, col : col + r.shape[1]] = lo
        col += r.shape[1]
    amp_h, amp_l = split(amps_ref[...].T)
    amp = jnp.concatenate([amp_h, amp_h, amp_l], axis=1)

    def gradient(t):
        part = dot(hal[...], vh_ref[t], NN)
        grad = own_ref[t] + part[:half] + part[half:] + dot(hal[0:half], vl_ref[t], NN)
        gh, gl = split(grad)
        grad_h[t] = gh
        grad_l[t] = gl
        for i in range(3):
            r = slice(i * modes, (i + 1) * modes)
            disp[t, i] = dot(amp, jnp.concatenate([gh[r], gl[r], gh[r]], axis=0), NN)

    def stress(t):
        for side in range(LANES // 128):
            e0 = t * LANES + side * 128
            lam = jnp.broadcast_to(lame_ref[0:1, e0 : e0 + 128], (16, 128)) * 0.5
            mu = jnp.broadcast_to(lame_ref[1:2, e0 : e0 + 128], (16, 128))
            at = [slice(j * LANES + side * 128, j * LANES + side * 128 + 128) for j in range(3)]
            for r0 in range(0, combos, 16):
                h = [[disp[t, i, r0 : r0 + 16, at[j]] for j in range(3)] for i in range(3)]
                s = {}
                for j in range(3):
                    for k in range(j, 3):
                        q = h[0][j] * h[0][k] + h[1][j] * h[1][k] + h[2][j] * h[2][k]
                        s[j, k] = (h[j][k] + h[k][j]) + q
                trace = lam * (s[0, 0] + s[1, 1] + s[2, 2])
                for j in range(3):
                    for k in range(j, 3):
                        v = mu * s[j, k]
                        v = v + trace if j == k else v
                        s[j, k] = s[k, j] = v
                for i in range(3):
                    for j in range(3):
                        p = s[i, j] + (h[i][0] * s[0, j] + h[i][1] * s[1, j] + h[i][2] * s[2, j])
                        hi, lo = split(p)
                        pio_ref[t, i * combos + r0 : i * combos + r0 + 16, at[j]] = hi
                        pio_ref[t, (3 + i) * combos + r0 : (3 + i) * combos + r0 + 16, at[j]] = lo

    def project(t, acc):
        for i in range(3):
            r = slice(i * modes, (i + 1) * modes)
            c = slice(i * combos, (i + 1) * combos)
            low = slice((3 + i) * combos, (4 + i) * combos)
            both = dot(jnp.concatenate([grad_h[t, r], grad_l[t, r]], axis=0), pio_ref[t, c, :], NT)
            acc = acc + both[:modes] + both[modes:] + dot(grad_h[t, r], pio_ref[t, low, :], NT)
        return acc

    acc = jnp.zeros((modes, combos), F32)
    gradient(0)
    for t in range(chunks):
        if t + 1 < chunks:
            gradient(t + 1)
        stress(t)
        acc = project(t, acc)
    modal_ref[...] = acc


def force_rows(pio_ref, wh_ref, wl_ref, t):
    half = pio_ref.shape[1] // 2
    part = dot(pio_ref[t], wh_ref[t], NT)
    return part[:half] + part[half:] + dot(pio_ref[t, 0:half, :], wl_ref[t], NT)


def halo_kernel(pio_ref, wh_ref, wl_ref, after_ref, *out_refs):
    del after_ref
    chunks = wh_ref.shape[0]
    for o in out_refs:
        o[...] = jnp.zeros_like(o)

    def chunk(t, carry):
        part = force_rows(pio_ref, wh_ref, wl_ref, t)
        col = 0
        for o in out_refs:
            o[...] += part[:, col : col + o.shape[1]]
            col += o.shape[1]
        return carry

    lax.fori_loop(0, chunks, chunk, 0)


def sum_kernel(a_ref, b_ref, after_ref, out_ref):
    del after_ref
    out_ref[...] = a_ref[...] + b_ref[...]


def own_kernel(pio_ref, wh_ref, wl_ref, after_ref, out_ref):
    del after_ref
    out_ref[...] = jnp.zeros_like(out_ref)

    def chunk(t, carry):
        out_ref[...] += force_rows(pio_ref, wh_ref, wl_ref, t)
        return carry

    lax.fori_loop(0, wh_ref.shape[0], chunk, 0)


def add_kernel(own_ref, hot_ref, a_ref, b_ref, c_ref, d_ref, out_hbm, back, out_s, sems):
    node_total = own_ref.shape[1]
    rows = own_ref.shape[0]
    combos = rows // 3
    col = 0
    for r in (a_ref, b_ref, c_ref, d_ref):
        hi, lo = split(r[...])
        back[0:rows, col : col + r.shape[1]] = hi
        back[rows:, col : col + r.shape[1]] = lo
        col += r.shape[1]
    copies = []
    for k in range(sems.shape[0]):
        width = node_total // sems.shape[0]
        at = slice(k * width, (k + 1) * width)
        part = dot(back[...], hot_ref[at, :], NT)
        for i in range(3):
            r = slice(i * combos, (i + 1) * combos)
            low = slice(rows + i * combos, rows + (i + 1) * combos)
            out_s[i, :, at] = own_ref[r, at] + part[r] + part[low]
        copies.append(pltpu.make_async_copy(out_s.at[:, :, at], out_hbm.at[:, :, at], sems.at[k]))
        copies[-1].start()
    for c in copies:
        c.wait()


def call(kernel, out_shape, args, scratch=(), vmem=24, hbm_in=(), any_in=(), any_out=False, flops=0):
    vm = pl.BlockSpec(memory_space=pltpu.VMEM)
    hbm = pl.BlockSpec(memory_space=pltpu.HBM)
    anywhere = pl.BlockSpec(memory_space=pl.ANY)
    many = isinstance(out_shape, (list, tuple))
    out = anywhere if any_out else vm
    args = [pltpu.with_memory_space_constraint(x, pltpu.HBM) if i in hbm_in else x for i, x in enumerate(args)]
    return pl.pallas_call(
        kernel,
        out_shape=out_shape,
        in_specs=[hbm if i in hbm_in else anywhere if i in any_in else vm for i in range(len(args))],
        out_specs=[out] * len(out_shape) if many else out,
        scratch_shapes=list(scratch),
        compiler_params=pltpu.CompilerParams(vmem_limit_bytes=vmem * MIB),
        cost_estimate=pl.CostEstimate(flops=flops, bytes_accessed=1 << 20, transcendentals=0),
    )(*args)


def local(amplitudes, mode_shapes, shape_grads, lame_params, connectivity, dom_sends, sector_sends):
    modes, _, node_total = mode_shapes.shape
    combos = amplitudes.shape[0]
    elems = connectivity.shape[1]
    dom_width, sec_width = dom_sends.shape[1], sector_sends.shape[1]
    chunks = elems // LANES
    cols = 3 * LANES
    sds = jax.ShapeDtypeStruct
    widths = (dom_width, dom_width, sec_width, sec_width)
    shapes = mode_shapes.transpose(1, 0, 2)
    grads = shape_grads.transpose(1, 0, 2)

    def exchange(a, b, c, d):
        return (
            swap(a, "dom", True, False),
            swap(b, "dom", False, False),
            swap(c, "sector", True, True),
            swap(d, "sector", False, True),
        )

    halo_width = sum(widths)
    *packets, hot, phi, grads_v, conn_v, lame_v = call(
        packet_kernel,
        [sds((3 * modes, w), F32) for w in widths]
        + [
            sds((node_total, halo_width), BF16),
            sds((6 * modes, node_total), BF16),
            sds(grads.shape, F32),
            sds(connectivity.shape, jnp.int32),
            sds(lame_params.shape, F32),
        ],
        (shapes, grads, connectivity, lame_params, dom_sends, sector_sends),
        scratch=[
            pltpu.VMEM(shapes.shape, F32),
            pltpu.VMEM(dom_sends.shape, jnp.int32),
            pltpu.VMEM(sector_sends.shape, jnp.int32),
            pltpu.SemaphoreType.DMA((6,)),
        ],
        hbm_in=range(6),
    )
    halo = exchange(*packets)
    wh, wl, vh, vl, own_grad = call(
        functools.partial(build_kernel, dom_width=dom_width, sec_width=sec_width),
        [sds((chunks, node_total, cols), BF16)] * 2
        + [sds((chunks, halo_width, cols), BF16)] * 2
        + [sds((chunks, 3 * modes, cols), F32)],
        (phi, conn_v, grads_v),
        scratch=[
            pltpu.VMEM((8, elems), jnp.int32),
            pltpu.VMEM((3, 8, elems), F32),
            pltpu.VMEM((8, 8, LANES), I16),
            pltpu.VMEM((24, 8, LANES), BF16),
            pltpu.VMEM((24, 8, LANES), BF16),
            pltpu.VMEM((8, LANES), I16),
            pltpu.SMEM((halo_width // sec_width,), jnp.int32),
        ],
        flops=6 * 3 * modes * node_total * 3 * elems,
    )
    pio, modal = call(
        element_kernel,
        [sds((chunks, 6 * combos, cols), BF16), sds((modes, combos), F32)],
        (amplitudes.T, lame_v, own_grad, *halo, vh, vl),
        scratch=[
            pltpu.VMEM((6 * modes, halo_width), BF16),
            pltpu.VMEM((chunks, 3, combos, cols), F32),
            pltpu.VMEM((chunks, 3 * modes, cols), BF16),
            pltpu.VMEM((chunks, 3 * modes, cols), BF16),
        ],
    )
    steps = []
    for axis in ("sector", "dom"):
        count = lax.axis_size(axis)
        step = 1
        while step < count:
            steps.append((axis, [(i, i ^ step) for i in range(count)]))
            step *= 2

    def other(x, k):
        return lax.ppermute(x, *steps[k])

    modal = modal + other(modal, 0)
    across = other(modal, 1)
    back = call(
        halo_kernel,
        [sds((3 * combos, w), F32) for w in widths],
        (pio, vh, vl, modal),
        any_in=(3,),
    )
    modal = call(sum_kernel, sds(modal.shape, F32), (modal, across, back[3]), any_in=(2,))
    modal = modal + other(modal, 2)
    returned = exchange(*back)
    own = call(
        own_kernel,
        sds((3 * combos, node_total), F32),
        (pio, wh, wl, modal),
        any_in=(3,),
        flops=6 * 3 * combos * node_total * 3 * elems,
    )
    forces = call(
        add_kernel,
        sds((3, combos, node_total), F32),
        (own, hot, *returned),
        scratch=[
            pltpu.VMEM((6 * combos, halo_width), BF16),
            pltpu.VMEM((3, combos, node_total), F32),
            pltpu.SemaphoreType.DMA((4,)),
        ],
        any_out=True,
    )
    for k in range(3, len(steps)):
        modal = modal + other(modal, k)
    all_nodes = node_total * lax.axis_size("sector") * lax.axis_size("dom")
    return forces.transpose(1, 0, 2), modal.T / math.sqrt(3.0 * all_nodes)


def solution(mesh):
    placed = (
        P(),
        P(None, None, ("sector", "dom")),
        P(None, None, ("sector", "dom")),
        P(None, ("sector", "dom")),
        P(None, ("sector", "dom")),
        P(None, ("sector", "dom")),
        P(None, ("sector", "dom")),
    )
    return jax.shard_map(
        local,
        mesh=mesh,
        in_specs=placed,
        out_specs=(P(None, None, ("sector", "dom")), P()),
        check_vma=False,
    )
```

```python
import functools
import math

import jax
import jax.numpy as jnp
from jax import lax
from jax.experimental import pallas as pl
from jax.experimental.pallas import tpu as pltpu
from jax.sharding import PartitionSpec as P

F32 = jnp.float32
BF16 = jnp.bfloat16
I16 = jnp.int16
MIB = 1 << 20
LANES = 256
NN = (((1,), (0,)), ((), ()))
NT = (((1,), (1,)), ((), ()))


def dot(a, b, dims):
    return lax.dot_general(a, b, dims, preferred_element_type=F32)


def split(x):
    hi = x.astype(BF16)
    return hi, (x - hi.astype(F32)).astype(BF16)


def partners(count, even_up):
    out = []
    for i in range(count):
        up = (i % 2 == 0) == even_up
        out.append((i, i + 1 if up else i - 1))
    return out


def swap(x, axis, even_up, closed):
    count = lax.axis_size(axis)
    pairs = [(i, j) for i, j in partners(count, even_up) if closed or 0 <= j < count]
    return lax.ppermute(x, axis, [(i, j % count) for i, j in pairs])


def parity():
    return lax.axis_index("dom") % 2, lax.axis_index("sector") % 2


def send_rows(dom_ref, sec_ref):
    dom_odd, sec_odd = (p == 1 for p in parity())
    d0, d1 = dom_ref[0:1, :], dom_ref[1:2, :]
    s0, s1 = sec_ref[0:1, :], sec_ref[1:2, :]
    return [
        jnp.where(dom_odd, d0, d1),
        jnp.where(dom_odd, d1, d0),
        jnp.where(sec_odd, s0, s1),
        jnp.where(sec_odd, s1, s0),
    ]


def one_hot(row, node_total):
    ids = lax.broadcasted_iota(jnp.int32, (node_total, row.shape[1]), 0)
    return jnp.where(ids == row, 1.0, 0.0).astype(BF16)


def packet_kernel(shapes_hbm, grads_hbm, conn_hbm, lame_hbm, dom_hbm, sec_hbm,
                  a_ref, b_ref, c_ref, d_ref, hot_ref, phi_ref, grads_ref, conn_ref, lame_ref,
                  shapes_ref, dom_ref, sec_ref, sems):
    pairs = [
        (dom_hbm, dom_ref),
        (sec_hbm, sec_ref),
        (shapes_hbm, shapes_ref),
        (grads_hbm, grads_ref),
        (conn_hbm, conn_ref),
        (lame_hbm, lame_ref),
    ]
    copies = [pltpu.make_async_copy(src, dst, sems.at[k]) for k, (src, dst) in enumerate(pairs)]
    for c in copies:
        c.start()
    node_total = shapes_ref.shape[2]
    modes = shapes_ref.shape[1]
    copies[0].wait()
    copies[1].wait()
    col = 0
    for row in send_rows(dom_ref, sec_ref):
        width = row.shape[1]
        hot_ref[:, col : col + width] = one_hot(row, node_total)
        col += width
    copies[2].wait()
    for i in range(3):
        hi, lo = split(shapes_ref[i])
        phi_ref[i * modes : (i + 1) * modes, :] = hi
        phi_ref[(3 + i) * modes : (4 + i) * modes, :] = lo
    half = 3 * modes
    col = 0
    for o in (a_ref, b_ref, c_ref, d_ref):
        width = o.shape[1]
        part = dot(phi_ref[...], hot_ref[:, col : col + width], NN)
        o[...] = part[:half] + part[half:]
        col += width
    for c in copies[3:]:
        c.wait()


def hold_kernel(x_ref, after_ref, out_ref):
    del x_ref, after_ref, out_ref


def build_kernel(phi_ref, conn_ref, grads_ref, *refs, dom_width, sec_width, chunks):
    wh, wl, vh, vl = (refs[k * chunks : (k + 1) * chunks] for k in range(4))
    own_ref, conn_s, grad_s, cs, ghs, gls, ios, phi_s, bases = refs[4 * chunks :]
    phi_s[...] = phi_ref[...]
    node_total = phi_ref.shape[1]
    half = phi_ref.shape[0] // 2
    conn = conn_ref[...]
    corner = lax.broadcasted_iota(jnp.int32, conn.shape, 0)
    grads = [grads_ref[j] for j in range(3)]
    total = list(grads)
    drop = jnp.zeros(conn.shape, jnp.bool_)
    for s in range(1, 8):
        same = pltpu.roll(conn, 8 - s, 0) == conn
        drop = drop | (same & (corner >= 8 - s))
        total = [t + jnp.where(same, pltpu.roll(g, 8 - s, 0), 0.0) for t, g in zip(total, grads)]
    conn_s[...] = jnp.where(drop, -1, conn)
    for j in range(3):
        grad_s[j] = total[j]
    ios[...] = lax.broadcasted_iota(jnp.int32, (8, LANES), 0).astype(I16)
    stretch = sec_width // 2
    run = 0
    first = node_total
    for width, odd in zip((dom_width, sec_width), parity()):
        for start in (first + (1 - odd) * width, first + odd * width):
            for k in range(width // stretch):
                bases[run] = start + k * stretch
                run += 1
        first += 2 * width
    for t in range(chunks):
        e0 = t * LANES
        for a in range(8):
            cs[t, a] = jnp.broadcast_to(conn_s[a : a + 1, e0 : e0 + LANES], (8, LANES)).astype(I16)
            for j in range(3):
                g = jnp.broadcast_to(grad_s[j, a : a + 1, e0 : e0 + LANES], (8, LANES))
                hi, lo = split(g)
                ghs[t, j * 8 + a] = hi
                gls[t, j * 8 + a] = lo

    def unit(hi_ref, lo_ref, t, row0, slot0):
        ids = ios[...] + slot0.astype(I16)
        hi = [jnp.zeros((8, LANES), BF16)] * 3
        lo = list(hi)
        for a in range(8):
            m = cs[t, a] == ids
            for j in range(3):
                hi[j] = jnp.where(m, ghs[t, j * 8 + a], hi[j])
                lo[j] = jnp.where(m, gls[t, j * 8 + a], lo[j])
        r = pl.ds(row0, 8)
        for j in range(3):
            hi_ref[r, j * LANES : (j + 1) * LANES] = hi[j]
            lo_ref[r, j * LANES : (j + 1) * LANES] = lo[j]

    own_units = 16
    for t in range(chunks):

        def own_rows(s, carry, t=t):
            row0 = pl.multiple_of(s * (8 * own_units), 8 * own_units)
            for u in range(own_units):
                unit(wh[t], wl[t], t, row0 + 8 * u, row0 + 8 * u)
            return carry

        lax.fori_loop(0, node_total // (8 * own_units), own_rows, 0)
        jobs = [(k, u) for k in range(run) for u in range(stretch // 8)]
        pieces = [(j, k, low) for j in range(3) for k in range(node_total // LANES) for low in (False, True)]
        done = 0
        for p, (j, k, low) in enumerate(pieces):
            col = slice(j * LANES, (j + 1) * LANES)
            rows = slice(k * LANES, (k + 1) * LANES)
            if low:
                part = dot(phi_s[0:half, rows], wl[t][rows, col], NN)
            else:
                part = dot(phi_s[:, rows], wh[t][rows, col], NN)
                part = part[:half] + part[half:]
            upto = len(jobs) * (p + 1) // len(pieces)
            for q, u in jobs[done:upto]:
                unit(vh[t], vl[t], t, q * stretch + 8 * u, bases[q] + 8 * u)
            done = upto
            if k == 0 and not low:
                own_ref[t, :, col] = part
            else:
                own_ref[t, :, col] += part


def element_kernel(amps_ref, lame_ref, own_ref, a_ref, b_ref, c_ref, d_ref, *refs, scale):
    chunks = own_ref.shape[0]
    vh, vl = refs[:chunks], refs[chunks : 2 * chunks]
    pio_ref, modal_ref, hal, disp, grad_h, grad_l = refs[2 * chunks :]
    modes, combos = amps_ref.shape
    half = 3 * modes
    col = 0
    for r in (a_ref, b_ref, c_ref, d_ref):
        hi, lo = split(r[...])
        hal[0:half, col : col + r.shape[1]] = hi
        hal[half:, col : col + r.shape[1]] = lo
        col += r.shape[1]
    amp_h, amp_l = split(amps_ref[...].T)
    amp = jnp.concatenate([amp_h, amp_h, amp_l], axis=1)

    def gradient(t):
        part = dot(hal[...], vh[t][...], NN)
        grad = own_ref[t] + part[:half] + part[half:] + dot(hal[0:half], vl[t][...], NN)
        gh, gl = split(grad)
        grad_h[t] = gh
        grad_l[t] = gl
        for i in range(3):
            r = slice(i * modes, (i + 1) * modes)
            disp[t, i] = dot(amp, jnp.concatenate([gh[r], gl[r], gh[r]], axis=0), NN)

    def stress(t):
        for side in range(LANES // 128):
            e0 = t * LANES + side * 128
            lam = jnp.broadcast_to(lame_ref[0:1, e0 : e0 + 128], (16, 128)) * 0.5
            mu = jnp.broadcast_to(lame_ref[1:2, e0 : e0 + 128], (16, 128))
            at = [slice(j * LANES + side * 128, j * LANES + side * 128 + 128) for j in range(3)]
            for r0 in range(0, combos, 16):
                h = [[disp[t, i, r0 : r0 + 16, at[j]] for j in range(3)] for i in range(3)]
                s = {}
                for j in range(3):
                    for k in range(j, 3):
                        q = h[0][j] * h[0][k] + h[1][j] * h[1][k] + h[2][j] * h[2][k]
                        s[j, k] = (h[j][k] + h[k][j]) + q
                trace = lam * (s[0, 0] + s[1, 1] + s[2, 2])
                for j in range(3):
                    for k in range(j, 3):
                        v = mu * s[j, k]
                        v = v + trace if j == k else v
                        s[j, k] = s[k, j] = v
                for i in range(3):
                    for j in range(3):
                        p = s[i, j] + (h[i][0] * s[0, j] + h[i][1] * s[1, j] + h[i][2] * s[2, j])
                        hi, lo = split(p)
                        pio_ref[t, i * combos + r0 : i * combos + r0 + 16, at[j]] = hi
                        pio_ref[t, (3 + i) * combos + r0 : (3 + i) * combos + r0 + 16, at[j]] = lo

    def project(t, acc):
        for i in range(3):
            r = slice(i * modes, (i + 1) * modes)
            c = slice(i * combos, (i + 1) * combos)
            low = slice((3 + i) * combos, (4 + i) * combos)
            both = dot(jnp.concatenate([grad_h[t, r], grad_l[t, r]], axis=0), pio_ref[t, c, :], NT)
            acc = acc + both[:modes] + both[modes:] + dot(grad_h[t, r], pio_ref[t, low, :], NT)
        return acc

    acc = jnp.zeros((modes, combos), F32)
    gradient(0)
    for t in range(chunks):
        if t + 1 < chunks:
            gradient(t + 1)
        stress(t)
        acc = project(t, acc)
    modal_ref[...] = acc * scale


def force_rows(pio_ref, wh, wl, t):
    half = pio_ref.shape[1] // 2
    part = dot(pio_ref[t], wh[t][...], NT)
    return part[:half] + part[half:] + dot(pio_ref[t, 0:half, :], wl[t][...], NT)


def halo_kernel(pio_ref, modal_ref, after_ref, *refs):
    del after_ref
    chunks, rows, _ = pio_ref.shape
    rows //= 2
    wh, wl, out_refs = refs[:chunks], refs[chunks : 2 * chunks], refs[2 * chunks :]
    for t in range(chunks):
        part = force_rows(pio_ref, wh, wl, t)
        col = 0
        for o in out_refs:
            piece = part[:, col : col + o.shape[1]]
            o[0:rows, :] = piece if t == 0 else o[0:rows, :] + piece
            col += o.shape[1]
    out_refs[2][rows:, 0 : modal_ref.shape[1]] = modal_ref[...]


def ride_kernel(sent_ref, got_ref, into_ref, out_ref, *, rows, combos):
    del into_ref
    out_ref[rows:, 0:combos] = sent_ref[rows:, 0:combos] + got_ref[rows:, 0:combos]


def land_kernel(sent_ref, got_ref, *refs, rows):
    out_ref = refs[-1]
    combos = out_ref.shape[1]
    out_ref[...] = sent_ref[rows:, 0:combos] + got_ref[rows:, 0:combos]


def sum_kernel(a_ref, b_ref, *refs):
    out_ref = refs[-1]
    out_ref[...] = a_ref[...] + b_ref[...]


def own_kernel(pio_ref, after_ref, *refs, first):
    del after_ref
    *before, out_ref = refs
    chunks = (len(before) - (first > 0)) // 2
    wh, wl = before[:chunks], before[chunks : 2 * chunks]
    for k in range(chunks):
        half = pio_ref.shape[1] // 2
        part = dot(pio_ref[first + k], wh[k][...], NT)
        part = part[:half] + part[half:] + dot(pio_ref[first + k, 0:half, :], wl[k][...], NT)
        if k == 0:
            out_ref[...] = part + before[-1][...] if first else part
        else:
            out_ref[...] += part


def add_kernel(own_ref, hot_ref, a_ref, b_ref, c_ref, d_ref, out_hbm, back, out_s, sems):
    node_total = own_ref.shape[1]
    rows = own_ref.shape[0]
    combos = rows // 3
    col = 0
    for r in (a_ref, b_ref, c_ref, d_ref):
        hi, lo = split(r[0:rows, :])
        back[0:rows, col : col + r.shape[1]] = hi
        back[rows:, col : col + r.shape[1]] = lo
        col += r.shape[1]
    copies = []
    for k in range(sems.shape[0]):
        width = node_total // sems.shape[0]
        at = slice(k * width, (k + 1) * width)
        part = dot(back[...], hot_ref[at, :], NT)
        for i in range(3):
            r = slice(i * combos, (i + 1) * combos)
            low = slice(rows + i * combos, rows + (i + 1) * combos)
            out_s[i, :, at] = own_ref[r, at] + part[r] + part[low]
        copies.append(pltpu.make_async_copy(out_s.at[:, :, at], out_hbm.at[:, :, at], sems.at[k]))
        copies[-1].start()
    for c in copies:
        c.wait()


def call(kernel, out_shape, args, scratch=(), vmem=24, hbm_in=(), any_in=(), any_out=False, flops=0, alias=None):
    vm = pl.BlockSpec(memory_space=pltpu.VMEM)
    hbm = pl.BlockSpec(memory_space=pltpu.HBM)
    anywhere = pl.BlockSpec(memory_space=pl.ANY)
    many = isinstance(out_shape, (list, tuple))
    out = anywhere if any_out else vm
    args = [pltpu.with_memory_space_constraint(x, pltpu.HBM) if i in hbm_in else x for i, x in enumerate(args)]
    return pl.pallas_call(
        kernel,
        out_shape=out_shape,
        in_specs=[hbm if i in hbm_in else anywhere if i in any_in else vm for i in range(len(args))],
        out_specs=[out] * len(out_shape) if many else out,
        scratch_shapes=list(scratch),
        input_output_aliases=alias or {},
        compiler_params=pltpu.CompilerParams(vmem_limit_bytes=vmem * MIB),
        cost_estimate=pl.CostEstimate(flops=flops, bytes_accessed=1 << 20, transcendentals=0),
    )(*args)


def local(amplitudes, mode_shapes, shape_grads, lame_params, connectivity, dom_sends, sector_sends):
    modes, _, node_total = mode_shapes.shape
    combos = amplitudes.shape[0]
    elems = connectivity.shape[1]
    dom_width, sec_width = dom_sends.shape[1], sector_sends.shape[1]
    chunks = elems // LANES
    cols = 3 * LANES
    sds = jax.ShapeDtypeStruct
    widths = (dom_width, dom_width, sec_width, sec_width)
    shapes = mode_shapes.transpose(1, 0, 2)
    grads = shape_grads.transpose(1, 0, 2)

    def exchange(a, b, c, d):
        return (
            swap(a, "dom", True, False),
            swap(b, "dom", False, False),
            swap(c, "sector", True, True),
            swap(d, "sector", False, True),
        )

    halo_width = sum(widths)
    *packets, hot, phi, grads_v, conn_v, lame_v = call(
        packet_kernel,
        [sds((3 * modes, w), F32) for w in widths]
        + [
            sds((node_total, halo_width), BF16),
            sds((6 * modes, node_total), BF16),
            sds(grads.shape, F32),
            sds(connectivity.shape, jnp.int32),
            sds(lame_params.shape, F32),
        ],
        (shapes, grads, connectivity, lame_params, dom_sends, sector_sends),
        scratch=[
            pltpu.VMEM(shapes.shape, F32),
            pltpu.VMEM(dom_sends.shape, jnp.int32),
            pltpu.VMEM(sector_sends.shape, jnp.int32),
            pltpu.SemaphoreType.DMA((6,)),
        ],
        hbm_in=range(6),
    )
    halo = exchange(*packets)
    *elem, own_grad = call(
        functools.partial(build_kernel, dom_width=dom_width, sec_width=sec_width, chunks=chunks),
        [sds((node_total, cols), BF16)] * (2 * chunks)
        + [sds((halo_width, cols), BF16)] * (2 * chunks)
        + [sds((chunks, 3 * modes, cols), F32)],
        (phi, conn_v, grads_v),
        scratch=[
            pltpu.VMEM((8, elems), jnp.int32),
            pltpu.VMEM((3, 8, elems), F32),
            pltpu.VMEM((chunks, 8, 8, LANES), I16),
            pltpu.VMEM((chunks, 24, 8, LANES), BF16),
            pltpu.VMEM((chunks, 24, 8, LANES), BF16),
            pltpu.VMEM((8, LANES), I16),
            pltpu.VMEM((6 * modes, node_total), BF16),
            pltpu.SMEM((2 * halo_width // sec_width,), jnp.int32),
        ],
        flops=6 * 3 * modes * node_total * 3 * elems,
    )
    all_nodes = node_total * lax.axis_size("sector") * lax.axis_size("dom")
    pio, modal = call(
        functools.partial(element_kernel, scale=1.0 / math.sqrt(3.0 * all_nodes)),
        [sds((chunks, 6 * combos, cols), BF16), sds((modes, combos), F32)],
        (amplitudes.T, lame_v, own_grad, *halo, *elem[2 * chunks :]),
        scratch=[
            pltpu.VMEM((6 * modes, halo_width), BF16),
            pltpu.VMEM((chunks, 3, combos, cols), F32),
            pltpu.VMEM((chunks, 3 * modes, cols), BF16),
            pltpu.VMEM((chunks, 3 * modes, cols), BF16),
        ],
    )
    rows = 3 * combos
    sector, dom = lax.axis_size("sector"), lax.axis_size("dom")

    def other(x, axis, step):
        return lax.ppermute(x, axis, [(i, i ^ step) for i in range(lax.axis_size(axis))])

    def fold(x, axis, step, *after, hbm_in=()):
        args = (x, other(x, axis, step), *after)
        anywhere = [i for i in range(2, len(args)) if i not in hbm_in]
        return call(sum_kernel, sds(x.shape, F32), args, any_in=anywhere, hbm_in=hbm_in)

    def scatter_own(first, last, after, before=()):
        return call(
            functools.partial(own_kernel, first=first),
            sds((rows, node_total), F32),
            (pio, after, *elem[first:last], *elem[chunks + first : chunks + last], *before),
            any_in=(1,),
            flops=2 * 3 * rows * node_total * 3 * LANES * (last - first),
        )

    own = scatter_own(0, 1, modal)
    modal = fold(modal, "dom", 1, own)
    ride = sector == 4
    heights = (rows, rows, rows + modes, rows + modes if ride else rows)
    back_a, back_b, back_c, back_d = call(
        halo_kernel,
        [sds((h, w), F32) for h, w in zip(heights, widths)],
        (pio, modal, own, *elem[2 * chunks :]),
        any_in=(2,),
    )
    got_c = swap(back_c, "sector", True, True)
    got_a = swap(back_a, "dom", True, False)
    if ride:
        back_d = call(
            functools.partial(ride_kernel, rows=rows, combos=combos),
            sds(back_d.shape, F32),
            (back_c, got_c, back_d),
            any_in=(2,),
            alias={2: 0},
        )
    got_d = swap(back_d, "sector", False, True)
    back_b = call(hold_kernel, sds(back_b.shape, F32), (back_b, back_d), any_in=(0, 1), any_out=True, alias={0: 0})
    got_b = swap(back_b, "dom", False, False)
    own = scatter_own(1, chunks - 1, back_d, (own,))
    landed = (back_d, got_d) if ride else (back_c, got_c)
    modal = call(
        functools.partial(land_kernel, rows=rows),
        sds(modal.shape, F32),
        (*landed, own),
        any_in=(2,),
    )
    own = scatter_own(chunks - 1, chunks, modal, (own,))
    step = 2
    while not ride and step < sector:
        modal = modal + other(modal, "sector", step)
        step *= 2
    step = 2
    while 4 * step <= dom:
        modal = fold(modal, "dom", step, own)
        step *= 2
    returned = (got_a, got_b, got_c, got_d)
    forces = call(
        add_kernel,
        sds((3, combos, node_total), F32),
        (own, hot, *returned),
        scratch=[
            pltpu.VMEM((6 * combos, halo_width), BF16),
            pltpu.VMEM((3, combos, node_total), F32),
            pltpu.SemaphoreType.DMA((4,)),
        ],
        any_out=True,
    )
    modal = fold(modal, "dom", dom // 2, forces, hbm_in=(2,))
    return forces.transpose(1, 0, 2), modal.T


def solution(mesh):
    placed = (
        P(),
        P(None, None, ("sector", "dom")),
        P(None, None, ("sector", "dom")),
        P(None, ("sector", "dom")),
        P(None, ("sector", "dom")),
        P(None, ("sector", "dom")),
        P(None, ("sector", "dom")),
    )
    return jax.shard_map(
        local,
        mesh=mesh,
        in_specs=placed,
        out_specs=(P(None, None, ("sector", "dom")), P()),
        check_vma=False,
    )
```

```python
import functools
import math

import jax
import jax.numpy as jnp
from jax import lax
from jax.experimental import pallas as pl
from jax.experimental.pallas import tpu as pltpu
from jax.sharding import PartitionSpec as P

F32 = jnp.float32
BF16 = jnp.bfloat16
I16 = jnp.int16
MIB = 1 << 20
LANES = 256
NN = (((1,), (0,)), ((), ()))
NT = (((1,), (1,)), ((), ()))


def dot(a, b, dims):
    return lax.dot_general(a, b, dims, preferred_element_type=F32)


def split(x):
    hi = x.astype(BF16)
    return hi, (x - hi.astype(F32)).astype(BF16)


def partners(count, even_up):
    out = []
    for i in range(count):
        up = (i % 2 == 0) == even_up
        out.append((i, i + 1 if up else i - 1))
    return out


def swap(x, axis, even_up, closed):
    count = lax.axis_size(axis)
    pairs = [(i, j) for i, j in partners(count, even_up) if closed or 0 <= j < count]
    return lax.ppermute(x, axis, [(i, j % count) for i, j in pairs])


def parity():
    return lax.axis_index("dom") % 2, lax.axis_index("sector") % 2


def send_rows(dom_ref, sec_ref):
    dom_odd, sec_odd = (p == 1 for p in parity())
    d0, d1 = dom_ref[0:1, :], dom_ref[1:2, :]
    s0, s1 = sec_ref[0:1, :], sec_ref[1:2, :]
    return [
        jnp.where(dom_odd, d0, d1),
        jnp.where(dom_odd, d1, d0),
        jnp.where(sec_odd, s0, s1),
        jnp.where(sec_odd, s1, s0),
    ]


def one_hot(row, node_total):
    ids = lax.broadcasted_iota(jnp.int32, (node_total, row.shape[1]), 0)
    return jnp.where(ids == row, 1.0, 0.0).astype(BF16)


def packet_kernel(shapes_hbm, grads_hbm, conn_hbm, lame_hbm, dom_hbm, sec_hbm,
                  a_ref, b_ref, c_ref, d_ref, hot_ref, phi_ref, grads_ref, conn_ref, lame_ref,
                  shapes_ref, dom_ref, sec_ref, sems):
    pairs = [
        (dom_hbm, dom_ref),
        (sec_hbm, sec_ref),
        (shapes_hbm, shapes_ref),
        (grads_hbm, grads_ref),
        (conn_hbm, conn_ref),
        (lame_hbm, lame_ref),
    ]
    copies = [pltpu.make_async_copy(src, dst, sems.at[k]) for k, (src, dst) in enumerate(pairs)]
    for c in copies:
        c.start()
    node_total = shapes_ref.shape[2]
    modes = shapes_ref.shape[1]
    copies[0].wait()
    copies[1].wait()
    col = 0
    for row in send_rows(dom_ref, sec_ref):
        width = row.shape[1]
        hot_ref[:, col : col + width] = one_hot(row, node_total)
        col += width
    copies[2].wait()
    for i in range(3):
        hi, lo = split(shapes_ref[i])
        phi_ref[i * modes : (i + 1) * modes, :] = hi
        phi_ref[(3 + i) * modes : (4 + i) * modes, :] = lo
    half = 3 * modes
    col = 0
    for o in (a_ref, b_ref, c_ref, d_ref):
        width = o.shape[1]
        part = dot(phi_ref[...], hot_ref[:, col : col + width], NN)
        o[...] = part[:half] + part[half:]
        col += width
    for c in copies[3:]:
        c.wait()


def hold_kernel(x_ref, after_ref, out_ref):
    del x_ref, after_ref, out_ref


def build_kernel(phi_ref, conn_ref, grads_ref, *refs, dom_width, sec_width, chunks):
    wh, wl, vh, vl = (refs[k * chunks : (k + 1) * chunks] for k in range(4))
    own_ref, conn_s, grad_s, cs, ghs, gls, ios, phi_s, bases = refs[4 * chunks :]
    phi_s[...] = phi_ref[...]
    node_total = phi_ref.shape[1]
    half = phi_ref.shape[0] // 2
    conn = conn_ref[...]
    corner = lax.broadcasted_iota(jnp.int32, conn.shape, 0)
    grads = [grads_ref[j] for j in range(3)]
    total = list(grads)
    drop = jnp.zeros(conn.shape, jnp.bool_)
    for s in range(1, 8):
        same = pltpu.roll(conn, 8 - s, 0) == conn
        drop = drop | (same & (corner >= 8 - s))
        total = [t + jnp.where(same, pltpu.roll(g, 8 - s, 0), 0.0) for t, g in zip(total, grads)]
    conn_s[...] = jnp.where(drop, -1, conn)
    for j in range(3):
        grad_s[j] = total[j]
    ios[...] = lax.broadcasted_iota(jnp.int32, (8, LANES), 0).astype(I16)
    stretch = sec_width // 2
    run = 0
    first = node_total
    for width, odd in zip((dom_width, sec_width), parity()):
        for start in (first + (1 - odd) * width, first + odd * width):
            for k in range(width // stretch):
                bases[run] = start + k * stretch
                run += 1
        first += 2 * width
    for t in range(chunks):
        e0 = t * LANES
        for a in range(8):
            cs[t, a] = jnp.broadcast_to(conn_s[a : a + 1, e0 : e0 + LANES], (8, LANES)).astype(I16)
            for j in range(3):
                g = jnp.broadcast_to(grad_s[j, a : a + 1, e0 : e0 + LANES], (8, LANES))
                hi, lo = split(g)
                ghs[t, j * 8 + a] = hi
                gls[t, j * 8 + a] = lo

    def unit(hi_ref, lo_ref, t, row0, slot0):
        ids = ios[...] + slot0.astype(I16)
        hi = [jnp.zeros((8, LANES), BF16)] * 3
        lo = list(hi)
        for a in range(8):
            m = cs[t, a] == ids
            for j in range(3):
                hi[j] = jnp.where(m, ghs[t, j * 8 + a], hi[j])
                lo[j] = jnp.where(m, gls[t, j * 8 + a], lo[j])
        r = pl.ds(row0, 8)
        for j in range(3):
            hi_ref[r, j * LANES : (j + 1) * LANES] = hi[j]
            lo_ref[r, j * LANES : (j + 1) * LANES] = lo[j]

    own_units = 16
    for t in range(chunks):

        def own_rows(s, carry, t=t):
            row0 = pl.multiple_of(s * (8 * own_units), 8 * own_units)
            for u in range(own_units):
                unit(wh[t], wl[t], t, row0 + 8 * u, row0 + 8 * u)
            return carry

        lax.fori_loop(0, node_total // (8 * own_units), own_rows, 0)
        jobs = [(k, u) for k in range(run) for u in range(stretch // 8)]
        pieces = [(j, k, low) for j in range(3) for k in range(node_total // LANES) for low in (False, True)]
        done = 0
        for p, (j, k, low) in enumerate(pieces):
            col = slice(j * LANES, (j + 1) * LANES)
            rows = slice(k * LANES, (k + 1) * LANES)
            if low:
                part = dot(phi_s[0:half, rows], wl[t][rows, col], NN)
            else:
                part = dot(phi_s[:, rows], wh[t][rows, col], NN)
                part = part[:half] + part[half:]
            upto = len(jobs) * (p + 1) // len(pieces)
            for q, u in jobs[done:upto]:
                unit(vh[t], vl[t], t, q * stretch + 8 * u, bases[q] + 8 * u)
            done = upto
            if k == 0 and not low:
                own_ref[t, :, col] = part
            else:
                own_ref[t, :, col] += part


def element_kernel(amps_ref, lame_ref, own_ref, a_ref, b_ref, c_ref, d_ref, *refs, scale):
    chunks = own_ref.shape[0]
    vh, vl = refs[:chunks], refs[chunks : 2 * chunks]
    pio_ref, modal_ref, hal, disp, grad_h, grad_l = refs[2 * chunks :]
    modes, combos = amps_ref.shape
    half = 3 * modes
    col = 0
    for r in (a_ref, b_ref, c_ref, d_ref):
        hi, lo = split(r[...])
        hal[0:half, col : col + r.shape[1]] = hi
        hal[half:, col : col + r.shape[1]] = lo
        col += r.shape[1]
    amp_h, amp_l = split(amps_ref[...].T)
    amp = jnp.concatenate([amp_h, amp_h, amp_l], axis=1)

    def gradient(t):
        part = dot(hal[...], vh[t][...], NN)
        grad = own_ref[t] + part[:half] + part[half:] + dot(hal[0:half], vl[t][...], NN)
        gh, gl = split(grad)
        grad_h[t] = gh
        grad_l[t] = gl
        for i in range(3):
            r = slice(i * modes, (i + 1) * modes)
            disp[t, i] = dot(amp, jnp.concatenate([gh[r], gl[r], gh[r]], axis=0), NN)

    def stress(t):
        for side in range(LANES // 128):
            e0 = t * LANES + side * 128
            lam = jnp.broadcast_to(lame_ref[0:1, e0 : e0 + 128], (16, 128)) * 0.5
            mu = jnp.broadcast_to(lame_ref[1:2, e0 : e0 + 128], (16, 128))
            at = [slice(j * LANES + side * 128, j * LANES + side * 128 + 128) for j in range(3)]
            for r0 in range(0, combos, 16):
                h = [[disp[t, i, r0 : r0 + 16, at[j]] for j in range(3)] for i in range(3)]
                s = {}
                for j in range(3):
                    for k in range(j, 3):
                        q = h[0][j] * h[0][k] + h[1][j] * h[1][k] + h[2][j] * h[2][k]
                        s[j, k] = (h[j][k] + h[k][j]) + q
                trace = lam * (s[0, 0] + s[1, 1] + s[2, 2])
                for j in range(3):
                    for k in range(j, 3):
                        v = mu * s[j, k]
                        v = v + trace if j == k else v
                        s[j, k] = s[k, j] = v
                for i in range(3):
                    for j in range(3):
                        p = s[i, j] + (h[i][0] * s[0, j] + h[i][1] * s[1, j] + h[i][2] * s[2, j])
                        hi, lo = split(p)
                        pio_ref[t, i * combos + r0 : i * combos + r0 + 16, at[j]] = hi
                        pio_ref[t, (3 + i) * combos + r0 : (3 + i) * combos + r0 + 16, at[j]] = lo

    def project(t, acc):
        for i in range(3):
            r = slice(i * modes, (i + 1) * modes)
            c = slice(i * combos, (i + 1) * combos)
            low = slice((3 + i) * combos, (4 + i) * combos)
            both = dot(jnp.concatenate([grad_h[t, r], grad_l[t, r]], axis=0), pio_ref[t, c, :], NT)
            acc = acc + both[:modes] + both[modes:] + dot(grad_h[t, r], pio_ref[t, low, :], NT)
        return acc

    acc = jnp.zeros((modes, combos), F32)
    gradient(0)
    for t in range(chunks):
        if t + 1 < chunks:
            gradient(t + 1)
        stress(t)
        acc = project(t, acc)
    modal_ref[...] = acc * scale


def force_rows(pio_ref, wh, wl, t):
    half = pio_ref.shape[1] // 2
    part = dot(pio_ref[t], wh[t][...], NT)
    return part[:half] + part[half:] + dot(pio_ref[t, 0:half, :], wl[t][...], NT)


def halo_kernel(pio_ref, *refs):
    chunks, rows, _ = pio_ref.shape
    rows //= 2
    wh, wl, out_refs = refs[:chunks], refs[chunks : 2 * chunks], refs[2 * chunks :]
    for t in range(chunks):
        part = force_rows(pio_ref, wh, wl, t)
        col = 0
        for o in out_refs:
            piece = part[:, col : col + o.shape[1]]
            o[0:rows, :] = piece if t == 0 else o[0:rows, :] + piece
            col += o.shape[1]


def board_kernel(a_ref, b_ref, into_ref, out_ref, *, rows):
    del into_ref
    out_ref[rows:, 0 : a_ref.shape[1]] = a_ref[...] + b_ref[...]


def ride_kernel(sent_ref, got_ref, into_ref, out_ref, *, rows, combos):
    del into_ref
    out_ref[rows:, 0:combos] = sent_ref[rows:, 0:combos] + got_ref[rows:, 0:combos]


def land_kernel(sent_ref, got_ref, *refs, rows):
    out_ref = refs[-1]
    combos = out_ref.shape[1]
    out_ref[...] = sent_ref[rows:, 0:combos] + got_ref[rows:, 0:combos]


def sum_kernel(a_ref, b_ref, *refs):
    out_ref = refs[-1]
    out_ref[...] = a_ref[...] + b_ref[...]


def own_kernel(pio_ref, after_ref, *refs, first):
    del after_ref
    *before, out_ref = refs
    chunks = (len(before) - (first > 0)) // 2
    wh, wl = before[:chunks], before[chunks : 2 * chunks]
    for k in range(chunks):
        half = pio_ref.shape[1] // 2
        part = dot(pio_ref[first + k], wh[k][...], NT)
        part = part[:half] + part[half:] + dot(pio_ref[first + k, 0:half, :], wl[k][...], NT)
        if k == 0:
            out_ref[...] = part + before[-1][...] if first else part
        else:
            out_ref[...] += part


def add_kernel(own_ref, hot_ref, a_ref, b_ref, c_ref, d_ref, out_hbm, back, out_s, sems):
    node_total = own_ref.shape[1]
    rows = own_ref.shape[0]
    combos = rows // 3
    col = 0
    for r in (a_ref, b_ref, c_ref, d_ref):
        hi, lo = split(r[0:rows, :])
        back[0:rows, col : col + r.shape[1]] = hi
        back[rows:, col : col + r.shape[1]] = lo
        col += r.shape[1]
    copies = []
    for k in range(sems.shape[0]):
        width = node_total // sems.shape[0]
        at = slice(k * width, (k + 1) * width)
        part = dot(back[...], hot_ref[at, :], NT)
        for i in range(3):
            r = slice(i * combos, (i + 1) * combos)
            low = slice(rows + i * combos, rows + (i + 1) * combos)
            out_s[i, :, at] = own_ref[r, at] + part[r] + part[low]
        copies.append(pltpu.make_async_copy(out_s.at[:, :, at], out_hbm.at[:, :, at], sems.at[k]))
        copies[-1].start()
    for c in copies:
        c.wait()


def call(kernel, out_shape, args, scratch=(), vmem=24, hbm_in=(), any_in=(), any_out=False, flops=0, alias=None):
    vm = pl.BlockSpec(memory_space=pltpu.VMEM)
    hbm = pl.BlockSpec(memory_space=pltpu.HBM)
    anywhere = pl.BlockSpec(memory_space=pl.ANY)
    many = isinstance(out_shape, (list, tuple))
    out = anywhere if any_out else vm
    args = [pltpu.with_memory_space_constraint(x, pltpu.HBM) if i in hbm_in else x for i, x in enumerate(args)]
    return pl.pallas_call(
        kernel,
        out_shape=out_shape,
        in_specs=[hbm if i in hbm_in else anywhere if i in any_in else vm for i in range(len(args))],
        out_specs=[out] * len(out_shape) if many else out,
        scratch_shapes=list(scratch),
        input_output_aliases=alias or {},
        compiler_params=pltpu.CompilerParams(vmem_limit_bytes=vmem * MIB),
        cost_estimate=pl.CostEstimate(flops=flops, bytes_accessed=1 << 20, transcendentals=0),
    )(*args)


def local(amplitudes, mode_shapes, shape_grads, lame_params, connectivity, dom_sends, sector_sends):
    modes, _, node_total = mode_shapes.shape
    combos = amplitudes.shape[0]
    elems = connectivity.shape[1]
    dom_width, sec_width = dom_sends.shape[1], sector_sends.shape[1]
    chunks = elems // LANES
    cols = 3 * LANES
    sds = jax.ShapeDtypeStruct
    widths = (dom_width, dom_width, sec_width, sec_width)
    shapes = mode_shapes.transpose(1, 0, 2)
    grads = shape_grads.transpose(1, 0, 2)

    def exchange(a, b, c, d):
        return (
            swap(a, "dom", True, False),
            swap(b, "dom", False, False),
            swap(c, "sector", True, True),
            swap(d, "sector", False, True),
        )

    halo_width = sum(widths)
    *packets, hot, phi, grads_v, conn_v, lame_v = call(
        packet_kernel,
        [sds((3 * modes, w), F32) for w in widths]
        + [
            sds((node_total, halo_width), BF16),
            sds((6 * modes, node_total), BF16),
            sds(grads.shape, F32),
            sds(connectivity.shape, jnp.int32),
            sds(lame_params.shape, F32),
        ],
        (shapes, grads, connectivity, lame_params, dom_sends, sector_sends),
        scratch=[
            pltpu.VMEM(shapes.shape, F32),
            pltpu.VMEM(dom_sends.shape, jnp.int32),
            pltpu.VMEM(sector_sends.shape, jnp.int32),
            pltpu.SemaphoreType.DMA((6,)),
        ],
        hbm_in=range(6),
    )
    halo = exchange(*packets)
    *elem, own_grad = call(
        functools.partial(build_kernel, dom_width=dom_width, sec_width=sec_width, chunks=chunks),
        [sds((node_total, cols), BF16)] * (2 * chunks)
        + [sds((halo_width, cols), BF16)] * (2 * chunks)
        + [sds((chunks, 3 * modes, cols), F32)],
        (phi, conn_v, grads_v),
        scratch=[
            pltpu.VMEM((8, elems), jnp.int32),
            pltpu.VMEM((3, 8, elems), F32),
            pltpu.VMEM((chunks, 8, 8, LANES), I16),
            pltpu.VMEM((chunks, 24, 8, LANES), BF16),
            pltpu.VMEM((chunks, 24, 8, LANES), BF16),
            pltpu.VMEM((8, LANES), I16),
            pltpu.VMEM((6 * modes, node_total), BF16),
            pltpu.SMEM((2 * halo_width // sec_width,), jnp.int32),
        ],
        flops=6 * 3 * modes * node_total * 3 * elems,
    )
    all_nodes = node_total * lax.axis_size("sector") * lax.axis_size("dom")
    pio, modal = call(
        functools.partial(element_kernel, scale=1.0 / math.sqrt(3.0 * all_nodes)),
        [sds((chunks, 6 * combos, cols), BF16), sds((modes, combos), F32)],
        (amplitudes.T, lame_v, own_grad, *halo, *elem[2 * chunks :]),
        scratch=[
            pltpu.VMEM((6 * modes, halo_width), BF16),
            pltpu.VMEM((chunks, 3, combos, cols), F32),
            pltpu.VMEM((chunks, 3 * modes, cols), BF16),
            pltpu.VMEM((chunks, 3 * modes, cols), BF16),
        ],
    )
    rows = 3 * combos
    sector, dom = lax.axis_size("sector"), lax.axis_size("dom")

    def other(x, axis, step):
        return lax.ppermute(x, axis, [(i, i ^ step) for i in range(lax.axis_size(axis))])

    def fold(x, axis, step, *after, hbm_in=()):
        args = (x, other(x, axis, step), *after)
        anywhere = [i for i in range(2, len(args)) if i not in hbm_in]
        return call(sum_kernel, sds(x.shape, F32), args, any_in=anywhere, hbm_in=hbm_in)

    def scatter_own(first, last, after, before=()):
        return call(
            functools.partial(own_kernel, first=first),
            sds((rows, node_total), F32),
            (pio, after, *elem[first:last], *elem[chunks + first : chunks + last], *before),
            any_in=(1,),
            flops=2 * 3 * rows * node_total * 3 * LANES * (last - first),
        )

    across = other(modal, "dom", 1)
    ride = sector == 4
    heights = (rows, rows, rows + modes, rows + modes if ride else rows)
    back_a, back_b, back_c, back_d = call(
        halo_kernel,
        [sds((h, w), F32) for h, w in zip(heights, widths)],
        (pio, *elem[2 * chunks :]),
        flops=3 * 2 * rows * halo_width * 3 * elems,
    )
    back_c = call(
        functools.partial(board_kernel, rows=rows),
        sds(back_c.shape, F32),
        (modal, across, back_c),
        any_in=(2,),
        alias={2: 0},
    )
    got_c = swap(back_c, "sector", True, True)
    got_a = swap(back_a, "dom", True, False)
    if ride:
        back_d = call(
            functools.partial(ride_kernel, rows=rows, combos=combos),
            sds(back_d.shape, F32),
            (back_c, got_c, back_d),
            any_in=(2,),
            alias={2: 0},
        )
    got_d = swap(back_d, "sector", False, True)
    back_b = call(hold_kernel, sds(back_b.shape, F32), (back_b, back_d), any_in=(0, 1), any_out=True, alias={0: 0})
    got_b = swap(back_b, "dom", False, False)
    own = scatter_own(0, chunks // 2, back_d)
    landed = (back_d, got_d) if ride else (back_c, got_c)
    modal = call(
        functools.partial(land_kernel, rows=rows),
        sds(modal.shape, F32),
        (*landed, own),
        any_in=(2,),
    )
    own = scatter_own(chunks // 2, chunks, modal, (own,))
    step = 2
    while not ride and step < sector:
        modal = modal + other(modal, "sector", step)
        step *= 2
    step = 2
    while 4 * step <= dom:
        modal = fold(modal, "dom", step, own)
        step *= 2
    returned = (got_a, got_b, got_c, got_d)
    forces = call(
        add_kernel,
        sds((3, combos, node_total), F32),
        (own, hot, *returned),
        scratch=[
            pltpu.VMEM((6 * combos, halo_width), BF16),
            pltpu.VMEM((3, combos, node_total), F32),
            pltpu.SemaphoreType.DMA((4,)),
        ],
        any_out=True,
    )
    modal = fold(modal, "dom", dom // 2, forces, hbm_in=(2,))
    return forces.transpose(1, 0, 2), modal.T


def solution(mesh):
    placed = (
        P(),
        P(None, None, ("sector", "dom")),
        P(None, None, ("sector", "dom")),
        P(None, ("sector", "dom")),
        P(None, ("sector", "dom")),
        P(None, ("sector", "dom")),
        P(None, ("sector", "dom")),
    )
    return jax.shard_map(
        local,
        mesh=mesh,
        in_specs=placed,
        out_specs=(P(None, None, ("sector", "dom")), P()),
        check_vma=False,
    )
```

```python
import functools
import math

import jax
import jax.numpy as jnp
from jax import lax
from jax.experimental import pallas as pl
from jax.experimental.pallas import tpu as pltpu
from jax.sharding import PartitionSpec as P

F32 = jnp.float32
BF16 = jnp.bfloat16
I16 = jnp.int16
MIB = 1 << 20
LANES = 256
NN = (((1,), (0,)), ((), ()))
NT = (((1,), (1,)), ((), ()))


def dot(a, b, dims):
    return lax.dot_general(a, b, dims, preferred_element_type=F32)


def split(x):
    hi = x.astype(BF16)
    return hi, (x - hi.astype(F32)).astype(BF16)


def partners(count, even_up):
    out = []
    for i in range(count):
        up = (i % 2 == 0) == even_up
        out.append((i, i + 1 if up else i - 1))
    return out


def swap(x, axis, even_up, closed):
    count = lax.axis_size(axis)
    pairs = [(i, j) for i, j in partners(count, even_up) if closed or 0 <= j < count]
    return lax.ppermute(x, axis, [(i, j % count) for i, j in pairs])


def parity():
    return lax.axis_index("dom") % 2, lax.axis_index("sector") % 2


def send_rows(dom_ref, sec_ref):
    dom_odd, sec_odd = (p == 1 for p in parity())
    d0, d1 = dom_ref[0:1, :], dom_ref[1:2, :]
    s0, s1 = sec_ref[0:1, :], sec_ref[1:2, :]
    return [
        jnp.where(dom_odd, d0, d1),
        jnp.where(dom_odd, d1, d0),
        jnp.where(sec_odd, s0, s1),
        jnp.where(sec_odd, s1, s0),
    ]


def one_hot(row, node_total):
    ids = lax.broadcasted_iota(jnp.int32, (node_total, row.shape[1]), 0)
    return jnp.where(ids == row, 1.0, 0.0).astype(BF16)


def packet_kernel(shapes_hbm, grads_hbm, conn_hbm, lame_hbm, dom_hbm, sec_hbm,
                  a_ref, b_ref, c_ref, d_ref, hot_ref, phi_ref, grads_ref, conn_ref, lame_ref,
                  shapes_ref, dom_ref, sec_ref, sems):
    pairs = [
        (dom_hbm, dom_ref),
        (sec_hbm, sec_ref),
        (shapes_hbm, shapes_ref),
        (grads_hbm, grads_ref),
        (conn_hbm, conn_ref),
        (lame_hbm, lame_ref),
    ]
    copies = [pltpu.make_async_copy(src, dst, sems.at[k]) for k, (src, dst) in enumerate(pairs)]
    for c in copies:
        c.start()
    node_total = shapes_ref.shape[2]
    modes = shapes_ref.shape[1]
    copies[0].wait()
    copies[1].wait()
    col = 0
    for row in send_rows(dom_ref, sec_ref):
        width = row.shape[1]
        hot_ref[:, col : col + width] = one_hot(row, node_total)
        col += width
    copies[2].wait()
    for i in range(3):
        hi, lo = split(shapes_ref[i])
        phi_ref[i * modes : (i + 1) * modes, :] = hi
        phi_ref[(3 + i) * modes : (4 + i) * modes, :] = lo
    half = 3 * modes
    col = 0
    for o in (a_ref, b_ref, c_ref, d_ref):
        width = o.shape[1]
        part = dot(phi_ref[...], hot_ref[:, col : col + width], NN)
        o[...] = part[:half] + part[half:]
        col += width
    for c in copies[3:]:
        c.wait()


def hold_kernel(x_ref, after_ref, out_ref):
    del x_ref, after_ref, out_ref


def build_kernel(phi_ref, conn_ref, grads_ref, *refs, dom_width, sec_width, chunks):
    wh, wl, vh, vl = (refs[k * chunks : (k + 1) * chunks] for k in range(4))
    own_ref, conn_s, grad_s, cs, ghs, gls, ios, phi_s, bases = refs[4 * chunks :]
    phi_s[...] = phi_ref[...]
    node_total = phi_ref.shape[1]
    half = phi_ref.shape[0] // 2
    conn = conn_ref[...]
    corner = lax.broadcasted_iota(jnp.int32, conn.shape, 0)
    grads = [grads_ref[j] for j in range(3)]
    total = list(grads)
    drop = jnp.zeros(conn.shape, jnp.bool_)
    for s in range(1, 8):
        same = pltpu.roll(conn, 8 - s, 0) == conn
        drop = drop | (same & (corner >= 8 - s))
        total = [t + jnp.where(same, pltpu.roll(g, 8 - s, 0), 0.0) for t, g in zip(total, grads)]
    conn_s[...] = jnp.where(drop, -1, conn)
    for j in range(3):
        grad_s[j] = total[j]
    ios[...] = lax.broadcasted_iota(jnp.int32, (8, LANES), 0).astype(I16)
    stretch = sec_width // 2
    run = 0
    first = node_total
    for width, odd in zip((dom_width, sec_width), parity()):
        for start in (first + (1 - odd) * width, first + odd * width):
            for k in range(width // stretch):
                bases[run] = start + k * stretch
                run += 1
        first += 2 * width
    for t in range(chunks):
        e0 = t * LANES
        for a in range(8):
            cs[t, a] = jnp.broadcast_to(conn_s[a : a + 1, e0 : e0 + LANES], (8, LANES)).astype(I16)
            for j in range(3):
                g = jnp.broadcast_to(grad_s[j, a : a + 1, e0 : e0 + LANES], (8, LANES))
                hi, lo = split(g)
                ghs[t, j * 8 + a] = hi
                gls[t, j * 8 + a] = lo

    def unit(hi_ref, lo_ref, t, row0, slot0):
        ids = ios[...] + slot0.astype(I16)
        hi = [jnp.zeros((8, LANES), BF16)] * 3
        lo = list(hi)
        for a in range(8):
            m = cs[t, a] == ids
            for j in range(3):
                hi[j] = jnp.where(m, ghs[t, j * 8 + a], hi[j])
                lo[j] = jnp.where(m, gls[t, j * 8 + a], lo[j])
        r = pl.ds(row0, 8)
        for j in range(3):
            hi_ref[r, j * LANES : (j + 1) * LANES] = hi[j]
            lo_ref[r, j * LANES : (j + 1) * LANES] = lo[j]

    own_units = 16
    for t in range(chunks):

        def own_rows(s, carry, t=t):
            row0 = pl.multiple_of(s * (8 * own_units), 8 * own_units)
            for u in range(own_units):
                unit(wh[t], wl[t], t, row0 + 8 * u, row0 + 8 * u)
            return carry

        lax.fori_loop(0, node_total // (8 * own_units), own_rows, 0)
        jobs = [(k, u) for k in range(run) for u in range(stretch // 8)]
        pieces = [(j, k, low) for j in range(3) for k in range(node_total // LANES) for low in (False, True)]
        done = 0
        for p, (j, k, low) in enumerate(pieces):
            col = slice(j * LANES, (j + 1) * LANES)
            rows = slice(k * LANES, (k + 1) * LANES)
            if low:
                part = dot(phi_s[0:half, rows], wl[t][rows, col], NN)
            else:
                part = dot(phi_s[:, rows], wh[t][rows, col], NN)
                part = part[:half] + part[half:]
            upto = len(jobs) * (p + 1) // len(pieces)
            for q, u in jobs[done:upto]:
                unit(vh[t], vl[t], t, q * stretch + 8 * u, bases[q] + 8 * u)
            done = upto
            if k == 0 and not low:
                own_ref[t, :, col] = part
            else:
                own_ref[t, :, col] += part


def element_kernel(amps_ref, lame_ref, own_ref, a_ref, b_ref, c_ref, d_ref, *refs, scale):
    chunks = own_ref.shape[0]
    vh, vl = refs[:chunks], refs[chunks : 2 * chunks]
    pio_ref, modal_ref, hal, disp, grad_h, grad_l = refs[2 * chunks :]
    modes, combos = amps_ref.shape
    half = 3 * modes
    col = 0
    for r in (a_ref, b_ref, c_ref, d_ref):
        hi, lo = split(r[...])
        hal[0:half, col : col + r.shape[1]] = hi
        hal[half:, col : col + r.shape[1]] = lo
        col += r.shape[1]
    amp_h, amp_l = split(amps_ref[...].T)
    amp = jnp.concatenate([amp_h, amp_h, amp_l], axis=1)

    def gradient(t):
        part = dot(hal[...], vh[t][...], NN)
        grad = own_ref[t] + part[:half] + part[half:] + dot(hal[0:half], vl[t][...], NN)
        gh, gl = split(grad)
        grad_h[t] = gh
        grad_l[t] = gl
        for i in range(3):
            r = slice(i * modes, (i + 1) * modes)
            disp[t, i] = dot(amp, jnp.concatenate([gh[r], gl[r], gh[r]], axis=0), NN)

    def stress(t):
        for side in range(LANES // 128):
            e0 = t * LANES + side * 128
            lam = jnp.broadcast_to(lame_ref[0:1, e0 : e0 + 128], (16, 128)) * 0.5
            mu = jnp.broadcast_to(lame_ref[1:2, e0 : e0 + 128], (16, 128))
            at = [slice(j * LANES + side * 128, j * LANES + side * 128 + 128) for j in range(3)]
            for r0 in range(0, combos, 16):
                h = [[disp[t, i, r0 : r0 + 16, at[j]] for j in range(3)] for i in range(3)]
                s = {}
                for j in range(3):
                    for k in range(j, 3):
                        q = h[0][j] * h[0][k] + h[1][j] * h[1][k] + h[2][j] * h[2][k]
                        s[j, k] = (h[j][k] + h[k][j]) + q
                trace = lam * (s[0, 0] + s[1, 1] + s[2, 2])
                for j in range(3):
                    for k in range(j, 3):
                        v = mu * s[j, k]
                        v = v + trace if j == k else v
                        s[j, k] = s[k, j] = v
                for i in range(3):
                    for j in range(3):
                        p = s[i, j] + (h[i][0] * s[0, j] + h[i][1] * s[1, j] + h[i][2] * s[2, j])
                        hi, lo = split(p)
                        pio_ref[t, i * combos + r0 : i * combos + r0 + 16, at[j]] = hi
                        pio_ref[t, (3 + i) * combos + r0 : (3 + i) * combos + r0 + 16, at[j]] = lo

    def project(t, acc):
        for i in range(3):
            r = slice(i * modes, (i + 1) * modes)
            c = slice(i * combos, (i + 1) * combos)
            low = slice((3 + i) * combos, (4 + i) * combos)
            both = dot(jnp.concatenate([grad_h[t, r], grad_l[t, r]], axis=0), pio_ref[t, c, :], NT)
            acc = acc + both[:modes] + both[modes:] + dot(grad_h[t, r], pio_ref[t, low, :], NT)
        return acc

    acc = jnp.zeros((modes, combos), F32)
    gradient(0)
    for t in range(chunks):
        if t + 1 < chunks:
            gradient(t + 1)
        stress(t)
        acc = project(t, acc)
    modal_ref[...] = acc * scale


def force_rows(pio_ref, wh, wl, t):
    half = pio_ref.shape[1] // 2
    part = dot(pio_ref[t], wh[t][...], NT)
    return part[:half] + part[half:] + dot(pio_ref[t, 0:half, :], wl[t][...], NT)


def halo_kernel(pio_ref, *refs):
    chunks, rows, _ = pio_ref.shape
    rows //= 2
    wh, wl, out_refs = refs[:chunks], refs[chunks : 2 * chunks], refs[2 * chunks :]
    for t in range(chunks):
        part = force_rows(pio_ref, wh, wl, t)
        col = 0
        for o in out_refs:
            piece = part[:, col : col + o.shape[1]]
            o[0:rows, :] = piece if t == 0 else o[0:rows, :] + piece
            col += o.shape[1]


def board_kernel(a_ref, b_ref, into_ref, out_ref, *, rows):
    del into_ref
    out_ref[rows:, 0 : a_ref.shape[1]] = a_ref[...] + b_ref[...]


def ride_kernel(sent_ref, got_ref, into_ref, out_ref, *, rows, combos):
    del into_ref
    out_ref[rows:, 0:combos] = sent_ref[rows:, 0:combos] + got_ref[rows:, 0:combos]


def land_kernel(sent_ref, got_ref, *refs, rows):
    out_ref = refs[-1]
    combos = out_ref.shape[1]
    out_ref[...] = sent_ref[rows:, 0:combos] + got_ref[rows:, 0:combos]


def sum_kernel(a_ref, b_ref, *refs):
    out_ref = refs[-1]
    out_ref[...] = a_ref[...] + b_ref[...]


def own_kernel(pio_ref, after_ref, *refs, first):
    del after_ref
    *before, out_ref = refs
    chunks = (len(before) - (first > 0)) // 2
    wh, wl = before[:chunks], before[chunks : 2 * chunks]
    for k in range(chunks):
        half = pio_ref.shape[1] // 2
        part = dot(pio_ref[first + k], wh[k][...], NT)
        part = part[:half] + part[half:] + dot(pio_ref[first + k, 0:half, :], wl[k][...], NT)
        if k == 0:
            out_ref[...] = part + before[-1][...] if first else part
        else:
            out_ref[...] += part


def rest_kernel(pio_ref, after_ref, hot_ref, c_ref, d_ref, *refs, first):
    own_kernel(pio_ref, after_ref, *refs, first=first)
    out_ref = refs[-1]
    rows = out_ref.shape[0]
    col = hot_ref.shape[1] - c_ref.shape[1] - d_ref.shape[1]
    for r in (c_ref, d_ref):
        both = jnp.concatenate(split(r[0:rows, :]), axis=0)
        part = dot(both, hot_ref[:, col : col + r.shape[1]], NT)
        out_ref[...] += part[:rows] + part[rows:]
        col += r.shape[1]


def add_kernel(own_ref, hot_ref, a_ref, b_ref, out_hbm, back, out_s, sems):
    node_total = own_ref.shape[1]
    rows = own_ref.shape[0]
    combos = rows // 3
    col = 0
    for r in (a_ref, b_ref):
        hi, lo = split(r[0:rows, :])
        back[0:rows, col : col + r.shape[1]] = hi
        back[rows:, col : col + r.shape[1]] = lo
        col += r.shape[1]
    copies = []
    for k in range(sems.shape[0]):
        width = node_total // sems.shape[0]
        at = slice(k * width, (k + 1) * width)
        part = dot(back[...], hot_ref[at, 0:col], NT)
        for i in range(3):
            r = slice(i * combos, (i + 1) * combos)
            low = slice(rows + i * combos, rows + (i + 1) * combos)
            out_s[i, :, at] = own_ref[r, at] + part[r] + part[low]
        copies.append(pltpu.make_async_copy(out_s.at[:, :, at], out_hbm.at[:, :, at], sems.at[k]))
        copies[-1].start()
    for c in copies:
        c.wait()


def call(kernel, out_shape, args, scratch=(), vmem=24, hbm_in=(), any_in=(), any_out=False, flops=0, alias=None):
    vm = pl.BlockSpec(memory_space=pltpu.VMEM)
    hbm = pl.BlockSpec(memory_space=pltpu.HBM)
    anywhere = pl.BlockSpec(memory_space=pl.ANY)
    many = isinstance(out_shape, (list, tuple))
    out = anywhere if any_out else vm
    args = [pltpu.with_memory_space_constraint(x, pltpu.HBM) if i in hbm_in else x for i, x in enumerate(args)]
    return pl.pallas_call(
        kernel,
        out_shape=out_shape,
        in_specs=[hbm if i in hbm_in else anywhere if i in any_in else vm for i in range(len(args))],
        out_specs=[out] * len(out_shape) if many else out,
        scratch_shapes=list(scratch),
        input_output_aliases=alias or {},
        compiler_params=pltpu.CompilerParams(vmem_limit_bytes=vmem * MIB),
        cost_estimate=pl.CostEstimate(flops=flops, bytes_accessed=1 << 20, transcendentals=0),
    )(*args)


def local(amplitudes, mode_shapes, shape_grads, lame_params, connectivity, dom_sends, sector_sends):
    modes, _, node_total = mode_shapes.shape
    combos = amplitudes.shape[0]
    elems = connectivity.shape[1]
    dom_width, sec_width = dom_sends.shape[1], sector_sends.shape[1]
    chunks = elems // LANES
    cols = 3 * LANES
    sds = jax.ShapeDtypeStruct
    widths = (dom_width, dom_width, sec_width, sec_width)
    shapes = mode_shapes.transpose(1, 0, 2)
    grads = shape_grads.transpose(1, 0, 2)

    def exchange(a, b, c, d):
        return (
            swap(a, "dom", True, False),
            swap(b, "dom", False, False),
            swap(c, "sector", True, True),
            swap(d, "sector", False, True),
        )

    halo_width = sum(widths)
    *packets, hot, phi, grads_v, conn_v, lame_v = call(
        packet_kernel,
        [sds((3 * modes, w), F32) for w in widths]
        + [
            sds((node_total, halo_width), BF16),
            sds((6 * modes, node_total), BF16),
            sds(grads.shape, F32),
            sds(connectivity.shape, jnp.int32),
            sds(lame_params.shape, F32),
        ],
        (shapes, grads, connectivity, lame_params, dom_sends, sector_sends),
        scratch=[
            pltpu.VMEM(shapes.shape, F32),
            pltpu.VMEM(dom_sends.shape, jnp.int32),
            pltpu.VMEM(sector_sends.shape, jnp.int32),
            pltpu.SemaphoreType.DMA((6,)),
        ],
        hbm_in=range(6),
    )
    halo = exchange(*packets)
    *elem, own_grad = call(
        functools.partial(build_kernel, dom_width=dom_width, sec_width=sec_width, chunks=chunks),
        [sds((node_total, cols), BF16)] * (2 * chunks)
        + [sds((halo_width, cols), BF16)] * (2 * chunks)
        + [sds((chunks, 3 * modes, cols), F32)],
        (phi, conn_v, grads_v),
        scratch=[
            pltpu.VMEM((8, elems), jnp.int32),
            pltpu.VMEM((3, 8, elems), F32),
            pltpu.VMEM((chunks, 8, 8, LANES), I16),
            pltpu.VMEM((chunks, 24, 8, LANES), BF16),
            pltpu.VMEM((chunks, 24, 8, LANES), BF16),
            pltpu.VMEM((8, LANES), I16),
            pltpu.VMEM((6 * modes, node_total), BF16),
            pltpu.SMEM((2 * halo_width // sec_width,), jnp.int32),
        ],
        flops=6 * 3 * modes * node_total * 3 * elems,
    )
    all_nodes = node_total * lax.axis_size("sector") * lax.axis_size("dom")
    pio, modal = call(
        functools.partial(element_kernel, scale=1.0 / math.sqrt(3.0 * all_nodes)),
        [sds((chunks, 6 * combos, cols), BF16), sds((modes, combos), F32)],
        (amplitudes.T, lame_v, own_grad, *halo, *elem[2 * chunks :]),
        scratch=[
            pltpu.VMEM((6 * modes, halo_width), BF16),
            pltpu.VMEM((chunks, 3, combos, cols), F32),
            pltpu.VMEM((chunks, 3 * modes, cols), BF16),
            pltpu.VMEM((chunks, 3 * modes, cols), BF16),
        ],
    )
    rows = 3 * combos
    sector, dom = lax.axis_size("sector"), lax.axis_size("dom")

    def other(x, axis, step):
        return lax.ppermute(x, axis, [(i, i ^ step) for i in range(lax.axis_size(axis))])

    def fold(x, axis, step, *after, hbm_in=()):
        args = (x, other(x, axis, step), *after)
        anywhere = [i for i in range(2, len(args)) if i not in hbm_in]
        return call(sum_kernel, sds(x.shape, F32), args, any_in=anywhere, hbm_in=hbm_in)

    def scatter_own(first, last, after, before=()):
        return call(
            functools.partial(own_kernel, first=first),
            sds((rows, node_total), F32),
            (pio, after, *elem[first:last], *elem[chunks + first : chunks + last], *before),
            any_in=(1,),
            flops=2 * 3 * rows * node_total * 3 * LANES * (last - first),
        )

    across = other(modal, "dom", 1)
    ride = sector == 4
    heights = (rows, rows, rows + modes, rows + modes if ride else rows)
    back_a, back_b, back_c, back_d = call(
        halo_kernel,
        [sds((h, w), F32) for h, w in zip(heights, widths)],
        (pio, *elem[2 * chunks :]),
        flops=3 * 2 * rows * halo_width * 3 * elems,
    )
    back_c = call(
        functools.partial(board_kernel, rows=rows),
        sds(back_c.shape, F32),
        (modal, across, back_c),
        any_in=(2,),
        alias={2: 0},
    )
    got_c = swap(back_c, "sector", True, True)
    got_a = swap(back_a, "dom", True, False)
    if ride:
        back_d = call(
            functools.partial(ride_kernel, rows=rows, combos=combos),
            sds(back_d.shape, F32),
            (back_c, got_c, back_d),
            any_in=(2,),
            alias={2: 0},
        )
    got_d = swap(back_d, "sector", False, True)
    back_b = call(hold_kernel, sds(back_b.shape, F32), (back_b, back_d), any_in=(0, 1), any_out=True, alias={0: 0})
    got_b = swap(back_b, "dom", False, False)
    own = scatter_own(0, chunks // 2, back_d)
    landed = (back_d, got_d) if ride else (back_c, got_c)
    modal = call(
        functools.partial(land_kernel, rows=rows),
        sds(modal.shape, F32),
        (*landed, own),
        any_in=(2,),
    )
    mid = chunks // 2
    own = call(
        functools.partial(rest_kernel, first=mid),
        sds((rows, node_total), F32),
        (pio, modal, hot, got_c, got_d, *elem[mid:chunks], *elem[chunks + mid : 2 * chunks], own),
        any_in=(1,),
        flops=2 * 3 * rows * node_total * 3 * LANES * (chunks - mid),
    )
    step = 2
    while not ride and step < sector:
        modal = modal + other(modal, "sector", step)
        step *= 2
    step = 2
    while 4 * step <= dom:
        modal = fold(modal, "dom", step, own)
        step *= 2
    returned = (got_a, got_b)
    forces = call(
        add_kernel,
        sds((3, combos, node_total), F32),
        (own, hot, *returned),
        scratch=[
            pltpu.VMEM((6 * combos, 2 * dom_width), BF16),
            pltpu.VMEM((3, combos, node_total), F32),
            pltpu.SemaphoreType.DMA((4,)),
        ],
        any_out=True,
    )
    modal = fold(modal, "dom", dom // 2, forces, hbm_in=(2,))
    return forces.transpose(1, 0, 2), modal.T


def solution(mesh):
    placed = (
        P(),
        P(None, None, ("sector", "dom")),
        P(None, None, ("sector", "dom")),
        P(None, ("sector", "dom")),
        P(None, ("sector", "dom")),
        P(None, ("sector", "dom")),
        P(None, ("sector", "dom")),
    )
    return jax.shard_map(
        local,
        mesh=mesh,
        in_specs=placed,
        out_specs=(P(None, None, ("sector", "dom")), P()),
        check_vma=False,
    )
```
